512 devices in a mesh: row: 128 (over x, y_lo, z, core), rep: 4 (over y_hi).
Axes of the slice: x: 4, y: 8 (y_hi: 4, y_lo: 2; y = y_hi * 2 + y_lo), z: 8, core: 2. Of those that a mesh axis runs over, the one named last changes fastest.
Arguments:
- pair: bfloat16 [1024, 1024, 128], P('row', 'rep'), may hold values from -6 to 6
- cotangent: bfloat16 [1024, 1024, 128], P('row', 'rep'), may hold values from -6 to 6
- token_mask: int32 [1024], replicated, may hold values 0 or 1
- in_gain: float32 [128], replicated, may hold values from 0.1 to 1.9
- in_bias: float32 [128], replicated, may hold values from -3 to 3
- proj_weight: bfloat16 [128, 640], replicated, may hold values from -0.5 to 0.5
- out_gain: float32 [128], replicated, may hold values from 0.1 to 1.9
- out_bias: float32 [128], replicated, may hold values from -3 to 3
- out_weight: bfloat16 [128, 128], replicated, may hold values from -0.5 to 0.5
Outputs:
- update: bfloat16 [1024, 1024, 128], P('row', 'rep')
- grad_pair: bfloat16 [1024, 1024, 128], P('row', 'rep')
- grad_proj_weight: float32 [128, 640], replicated
- grad_out_weight: float32 [128, 128], replicated
- grad_in_norm: float32 [2, 128], replicated
- grad_out_norm: float32 [2, 128], replicated
The draws below stay inside these ranges and needn't reach their ends.
All inputs are finite; a program needn't handle non-finite values.
Results may differ from the reference program's by a relative error of at most 0.0072.
Values may be sent and summed in bfloat16 or wider, within the bound.
A program may use at most 64 MiB of HBM per device.

```python
import jax
import jax.numpy as jnp
from jax import lax

N = 1024
C = 128
CH = 128


def place_ends(result, key, smallest, largest):
    shape = result.shape
    place = [jax.random.randint(jax.random.fold_in(key, axis), (), 0, shape[axis]) for axis in range(len(shape))]
    result = result.at[tuple(place)].set(smallest)
    longest = shape.index(max(shape))
    place[longest] = (place[longest] + 1) % shape[longest]
    return result.at[tuple(place)].set(largest)


def steps_of(stream_key, dims, cuts, smallest, high):
    factor_of = 1.0
    for position, blocks in cuts:
        steps = jax.random.uniform(jax.random.fold_in(jax.random.fold_in(stream_key, 6), position), (blocks,), jnp.float32, smallest / len(cuts), high / len(cuts))
        factor_of = factor_of * jnp.repeat(jnp.exp(steps), dims[position] // blocks).reshape((-1,) + (1,) * (len(dims) - 1 - position))
    return factor_of


def gaussian(key, dims, deviation, bound, pieces=(), held_as=jnp.bfloat16):
    gain = steps_of(key, dims, pieces, -0.22, 0.18) if pieces else 1.0
    values = jax.random.normal(key, dims, jnp.float32) * deviation * gain
    return jnp.minimum(jnp.maximum(values, -bound), bound).astype(held_as)


def setup_inputs(seed: int = 0) -> dict:
    splits = jax.random.split(jax.random.key(seed), 10)
    pair = gaussian(splits[0], (N, N, C), 1.0, 6.0, ((0, 128), (1, 4)))
    cotangent = gaussian(splits[1], (N, N, C), 1.0, 6.0, ((0, 128), (1, 4)))
    token_mask = place_ends((jax.random.randint(splits[2], (N,), 0, 8) < 7).astype(jnp.int32), jax.random.fold_in(splits[2], 1), 0, 1)
    in_gain = jnp.clip(1.0 + 0.18 * jax.random.normal(splits[3], (C,), jnp.float32), 0.1, 1.9)
    in_bias = gaussian(splits[4], (C,), 0.5, 3.0, (), jnp.float32)
    proj_weight = gaussian(splits[5], (C, 4 * CH + C), C ** -0.5, 0.5)
    out_gain = jnp.clip(1.0 + 0.18 * jax.random.normal(splits[6], (CH,), jnp.float32), 0.1, 1.9)
    out_bias = gaussian(splits[7], (CH,), 0.5, 3.0, (), jnp.float32)
    out_weight = gaussian(splits[8], (CH, C), CH ** -0.5, 0.5)
    return {"pair": pair, "cotangent": cotangent, "token_mask": token_mask, "in_gain": in_gain, "in_bias": in_bias, "proj_weight": proj_weight, "out_gain": out_gain, "out_bias": out_bias, "out_weight": out_weight}


EPSILON = 1e-05

def norm_forward(values, gain_vec, bias_vec):
    average = lax.optimization_barrier(jnp.mean(values, axis=-1, keepdims=True))
    centred = values - average
    inv_std = lax.rsqrt(lax.optimization_barrier(jnp.mean(centred * centred, axis=-1, keepdims=True)) + EPSILON)
    normed = centred * inv_std
    return (normed * gain_vec + bias_vec, normed, inv_std)

def norm_backward(upward, normed, inv_std, gain_vec):
    scaled = upward * gain_vec
    return inv_std * (scaled - lax.optimization_barrier(jnp.mean(scaled, axis=-1, keepdims=True)) - normed * lax.optimization_barrier(jnp.mean(scaled * normed, axis=-1, keepdims=True)))

def row_blocks(array):
    return array.reshape((array.shape[0] // 64, 64) + array.shape[1:])

def whole_rows(array):
    return array.reshape((array.shape[0] * array.shape[1],) + array.shape[2:])

def reference(pair, cotangent, token_mask, in_gain, in_bias, proj_weight, out_gain, out_bias, out_weight):
    mask_f = token_mask.astype(jnp.float32)
    w_ab = proj_weight[:, :4 * CH]
    w_gate = proj_weight[:, 4 * CH:]

    def project(z_blk, m_blk):
        normed_in, z_hat, z_inv = norm_forward(z_blk.astype(jnp.float32), in_gain, in_bias)
        norm_bf = normed_in.astype(jnp.bfloat16)
        flat_zn = norm_bf.reshape(-1, C)
        height = z_blk.shape[0]
        proj = jnp.dot(flat_zn, w_ab, preferred_element_type=jnp.float32).reshape(height, N, 4 * CH)
        gate_pre = jnp.dot(flat_zn, w_gate, preferred_element_type=jnp.float32).reshape(height, N, C)
        pair_mask = (m_blk[:, None] * mask_f[None, :])[:, :, None]
        return (flat_zn, z_hat, z_inv, proj, jax.nn.sigmoid(gate_pre), pair_mask)

    def front(packed):
        z_blk, m_blk = packed
        _, _, _, proj, _, pair_mask = project(z_blk, m_blk)
        left_value, left_gate, right_value, right_gate = jnp.split(proj, 4, axis=-1)
        left = (pair_mask * jax.nn.sigmoid(left_gate) * left_value).astype(jnp.bfloat16)
        right = (pair_mask * jax.nn.sigmoid(right_gate) * right_value).astype(jnp.bfloat16)
        return (left, right)
    left, right = lax.map(front, (row_blocks(pair), row_blocks(mask_f)))
    left_t = jnp.moveaxis(whole_rows(left), 2, 0)
    right_t = jnp.moveaxis(whole_rows(right), 2, 0)

    def channel_product(packed):
        left_m, right_m = packed
        return jnp.dot(left_m, right_m.T, preferred_element_type=jnp.float32).astype(jnp.bfloat16)
    tri = jnp.moveaxis(lax.map(channel_product, (left_t, right_t)), 0, 2)

    def middle(packed):
        z_blk, m_blk, x_blk, c_blk = packed
        _, _, _, _, gating, _ = project(z_blk, m_blk)
        height = z_blk.shape[0]
        xn, x_hat, x_inv = norm_forward(x_blk.astype(jnp.float32), out_gain, out_bias)
        flat_xn = xn.astype(jnp.bfloat16).reshape(-1, CH)
        projected = jnp.dot(flat_xn, out_weight, preferred_element_type=jnp.float32).reshape(height, N, C)
        update = (gating * projected).astype(jnp.bfloat16)
        upstream = c_blk.astype(jnp.float32)
        d_proj_out = (upstream * gating).astype(jnp.bfloat16)
        d_gate = (upstream * projected * gating * (1.0 - gating)).astype(jnp.bfloat16)
        flat_dy = d_proj_out.reshape(-1, C)
        grad_wo = jnp.dot(flat_xn.T, flat_dy, preferred_element_type=jnp.float32)
        d_xn = jnp.dot(flat_dy, out_weight.T, preferred_element_type=jnp.float32).reshape(height, N, CH)
        norm_terms = jnp.stack([lax.optimization_barrier(jnp.sum(d_xn * x_hat, axis=(0, 1))), lax.optimization_barrier(jnp.sum(d_xn, axis=(0, 1)))])
        d_tri = norm_backward(d_xn, x_hat, x_inv, out_gain).astype(jnp.bfloat16)
        return (update, d_gate, d_tri, grad_wo, norm_terms)
    update, d_gate, d_tri, wo_parts, out_norm_parts = lax.map(middle, (row_blocks(pair), row_blocks(mask_f), row_blocks(tri), row_blocks(cotangent)))
    d_tri_t = jnp.moveaxis(whole_rows(d_tri), 2, 0)

    def channel_grads(packed):
        d_mat, left_m, right_m = packed
        d_left = jnp.dot(d_mat, right_m, preferred_element_type=jnp.float32).astype(jnp.bfloat16)
        d_right = jnp.dot(d_mat.T, left_m, preferred_element_type=jnp.float32).astype(jnp.bfloat16)
        return (d_left, d_right)
    d_left_t, d_right_t = lax.map(channel_grads, (d_tri_t, left_t, right_t))
    d_left = jnp.moveaxis(d_left_t, 0, 2)
    d_right = jnp.moveaxis(d_right_t, 0, 2)

    def back(packed):
        z_blk, m_blk, dl_blk, dr_blk, dg_blk = packed
        flat_zn, z_hat, z_inv, proj, _, pair_mask = project(z_blk, m_blk)
        height = z_blk.shape[0]
        left_value, left_gate, right_value, right_gate = jnp.split(proj, 4, axis=-1)
        left_sig = jax.nn.sigmoid(left_gate)
        right_sig = jax.nn.sigmoid(right_gate)
        d_lm = dl_blk.astype(jnp.float32) * pair_mask
        d_rm = dr_blk.astype(jnp.float32) * pair_mask
        d_proj = jnp.concatenate([d_lm * left_sig, d_lm * left_value * left_sig * (1.0 - left_sig), d_rm * right_sig, d_rm * right_value * right_sig * (1.0 - right_sig)], axis=-1).astype(jnp.bfloat16)
        flat_dp = d_proj.reshape(-1, 4 * CH)
        flat_dg = dg_blk.reshape(-1, C)
        grad_wp = jnp.concatenate([jnp.dot(flat_zn.T, flat_dp, preferred_element_type=jnp.float32), jnp.dot(flat_zn.T, flat_dg, preferred_element_type=jnp.float32)], axis=1)
        d_normed = (jnp.dot(flat_dp, w_ab.T, preferred_element_type=jnp.float32) + jnp.dot(flat_dg, w_gate.T, preferred_element_type=jnp.float32)).reshape(height, N, C)
        norm_terms = jnp.stack([lax.optimization_barrier(jnp.sum(d_normed * z_hat, axis=(0, 1))), lax.optimization_barrier(jnp.sum(d_normed, axis=(0, 1)))])
        d_pair = norm_backward(d_normed, z_hat, z_inv, in_gain).astype(jnp.bfloat16)
        return (d_pair, grad_wp, norm_terms)
    grad_pair, wp_parts, in_norm_parts = lax.map(back, (row_blocks(pair), row_blocks(mask_f), row_blocks(d_left), row_blocks(d_right), d_gate))
    factor = 1.0 / N
    return (whole_rows(update), whole_rows(grad_pair), lax.optimization_barrier(jnp.sum(wp_parts, axis=0)) * factor, lax.optimization_barrier(jnp.sum(wo_parts, axis=0)) * factor, lax.optimization_barrier(jnp.sum(in_norm_parts, axis=0)) * factor, lax.optimization_barrier(jnp.sum(out_norm_parts, axis=0)) * factor)
```

```python
import functools
import types

import jax
import jax.numpy as jnp
from jax import lax
from jax.experimental import pallas as pl
from jax.experimental.pallas import tpu as pltpu
from jax.sharding import PartitionSpec as P

EPSILON = 1e-05
MESH = pl.DeviceIdType.MESH
NX, NY, NZ = 4, 8, 8


def coordinates():
    row, rep = lax.axis_index("row"), lax.axis_index("rep")
    return row // 32, rep * 2 + (row // 16) % 2, (row // 2) % 8, row % 2


def device_at(x, y, z, core):
    return (((x * 2 + y % 2) * 8 + z) * 2 + core, y // 2)


def remote(src, dst, send_sem, recv_sem, target):
    return pltpu.make_async_remote_copy(
        src, dst, send_sem, recv_sem, device_id=target, device_id_type=MESH
    )


def copy_to(src, dst, send_sem, recv_sem, target, me):
    same = jnp.logical_and(target[0] == me[0], target[1] == me[1])

    @pl.when(same)
    def _():
        pltpu.make_async_copy(src, dst, recv_sem).start()

    @pl.when(jnp.logical_not(same))
    def _():
        remote(src, dst, send_sem, recv_sem, target).start()


def wait_for(ref, sem):
    pltpu.make_async_copy(ref, ref, sem).wait()


def send_to_owners(send, place, send_sem, recv_sem):
    x, y, z, core = coordinates()
    me = (lax.axis_index("row"), lax.axis_index("rep"))
    sign = 1 - 2 * core

    def step(s, carry):
        dz, dy, dx = s % 8, (s // 8) % 8, s // 64
        hx = (x // 2 + dx) % 2
        ty, tz = (y + sign * dy + 8) % 8, (z + sign * dz + 8) % 8
        h = hx * 64 + ty * 8 + tz
        copy_to(send.at[h], place, send_sem, recv_sem, device_at(2 * hx, ty, tz, x // 2), me)
        return carry

    lax.fori_loop(0, 128, step, 0)


def finish_sends(send, send_sem):
    x, y, z, core = coordinates()
    keeps = jnp.logical_and(x % 2 == 0, core == x // 2)

    @pl.when(keeps)
    def _():
        wait_for(send.at[pl.ds(0, 127)], send_sem)

    @pl.when(jnp.logical_not(keeps))
    def _():
        wait_for(send, send_sem)


def aligned(start, unit):
    return pl.multiple_of(start, unit)


def unpack(slots):
    wide = slots.astype(jnp.float32)
    low, high = wide[:, :8].reshape(512, 128), wide[:, 8:].reshape(512, 128)
    return jnp.concatenate([low, high], axis=1)


def pack(block):
    low, high = block[:, :128].reshape(64, 8, 128), block[:, 128:].reshape(64, 8, 128)
    return jnp.concatenate([low, high], axis=1).astype(jnp.bfloat16).reshape(2, 32, 16, 128)


def dot(a, b, contract):
    return lax.dot_general(a, b, ((contract[0], contract[1]), ((), ())), preferred_element_type=jnp.float32)


def turn(q, sign, rep):
    return (rep + sign * q + 4) % 4


def start_hop(send, stage, part, hop_send, hop_recv):
    x, y, z, core = coordinates()
    me = (lax.axis_index("row"), lax.axis_index("rep"))
    rows = pl.ds(aligned(part * 32, 32), 32)
    for bx in range(2):
        target = device_at(2 * core + bx, y, z, x // 2)
        copy_to(send.at[bx, rows], stage.at[rows], hop_send, hop_recv.at[part], target, me)


def finish_hop(send, hop_send):
    x, y, z, core = coordinates()

    @pl.when(core == x // 2)
    def _():
        wait_for(send.at[0], hop_send)

    @pl.when(core != x // 2)
    def _():
        wait_for(send, hop_send)


def spread(stage, recv, hop_recv, send_sem, recv_sem):
    x, y, z, core = coordinates()
    rep = lax.axis_index("rep")
    me = (lax.axis_index("row"), rep)
    h = core * 64 + y * 8 + z
    sign = 1 - 2 * core

    def one_part(q, carry):
        part = turn(q, sign, rep)
        wait_for(stage.at[pl.ds(aligned(part * 32, 32), 32)], hop_recv.at[part])

        def step(s, carry):
            tc, dz, dy = (s + core) % 2, (s // 2) % 8, s // 16
            ty, tz = part * 2 + (y + dy) % 2, (z + sign * dz + 8) % 8
            place = part * 32 + (ty % 2) * 16 + tz * 2 + tc
            copy_to(stage.at[place], recv.at[h], send_sem, recv_sem, device_at(x, ty, tz, tc), me)
            return carry

        lax.fori_loop(0, 32, step, 0)
        return carry

    lax.fori_loop(0, 4, one_part, 0)


def rows_of(ref, row):
    return ref[pl.ds(row, 128, stride=16), :]


def load_row(ref, i):
    return jnp.concatenate([rows_of(ref, i), rows_of(ref, 8 + i)], axis=1)


def store_row(ref, i, value):
    ref[pl.ds(i, 128, stride=16), :] = value[:, :128]
    ref[pl.ds(8 + i, 128, stride=16), :] = value[:, 128:]


def mean0(value):
    return jnp.sum(value, axis=0, keepdims=True) * (1.0 / value.shape[0])


def standardize(value):
    centred = value - mean0(value)
    inv_std = lax.rsqrt(mean0(centred * centred) + EPSILON)
    return centred * inv_std, inv_std


def standardize_back(scaled, normed, inv_std):
    return inv_std * (scaled - mean0(scaled) - normed * mean0(scaled * normed))


def wide(column):
    return jnp.concatenate([column, column], axis=1)


NN, NT = ((1,), (0,)), ((1,), (1,))


def front_row(r, i):
    z_hat, z_inv = standardize(r.pair[i].astype(jnp.float32).T)
    r.z_hat[i] = z_hat
    r.z_inv[pl.ds(i, 1)] = z_inv
    normed = (z_hat * wide(r.in_gain[...]) + wide(r.in_bias[...])).astype(jnp.bfloat16)
    r.normed[i] = normed
    proj = dot(r.proj_t[...], normed, NN)
    mask = r.mask[pl.ds(i, 1)]
    for t, rows in ((0, r.rows_a), (1, r.rows_b)):
        value, gate = proj[t * 256 : t * 256 + 128], proj[t * 256 + 128 : t * 256 + 256]
        sig = jax.nn.sigmoid(gate)
        r.value[i, t] = value
        r.sig[i, t] = sig
        store_row(rows, i, mask * sig * value)
    r.gating[i] = jax.nn.sigmoid(proj[512:])


def middle_row(r, i):
    x_hat, x_inv = standardize(load_row(r.rows_a, i))
    gain = wide(r.out_gain[...])
    xn = (x_hat * gain + wide(r.out_bias[...])).astype(jnp.bfloat16)
    r.xn[i] = xn
    projected = dot(r.out_t[...], xn, NN)
    gating, upstream = r.gating[i], r.upstream[i]
    r.update_t[i] = gating * projected
    d_proj_out = (upstream * gating).astype(jnp.bfloat16)
    r.d_proj_out[i] = d_proj_out
    r.d_proj[i, pl.ds(512, 128)] = (upstream * projected * gating * (1.0 - gating)).astype(jnp.bfloat16)
    d_xn = dot(r.out_w[...], d_proj_out, NN)
    r.out_scale[...] += d_xn * x_hat
    r.out_shift[...] += d_xn
    store_row(r.rows_b, i, standardize_back(d_xn * gain, x_hat, x_inv))


def back_row(r, i):
    mask = r.mask[pl.ds(i, 1)]
    for t, rows in ((0, r.rows_a), (1, r.rows_b)):
        d_factor = load_row(rows, i) * mask
        value, sig = r.value[i, t], r.sig[i, t]
        r.d_proj[i, pl.ds(t * 256, 128)] = (d_factor * sig).astype(jnp.bfloat16)
        r.d_proj[i, pl.ds(t * 256 + 128, 128)] = (d_factor * value * sig * (1.0 - sig)).astype(jnp.bfloat16)
    d_proj = r.d_proj[i]
    r.part[pl.ds(0, 640)] += dot(d_proj, r.normed[i], NT)
    d_normed = dot(r.proj_w[...], d_proj, NN)
    r.d_normed[i] = d_normed
    r.in_scale[...] += d_normed * r.z_hat[i]
    r.in_shift[...] += d_normed


def grad_row(r, i):
    scaled = r.d_normed[i] * wide(r.in_gain[...])
    result = standardize_back(scaled, r.z_hat[i], r.z_inv[pl.ds(i, 1)])
    r.grad_pair[i] = result.T.astype(jnp.bfloat16)


def over_rows(function, r):
    def step(i, carry):
        function(r, i)
        return carry

    lax.fori_loop(0, 8, step, 0)


def to_f32_rows(rows, tiles):
    rows[...] = tiles.astype(jnp.float32).reshape(2048, 128)


def to_tiles(rows):
    return rows[...].astype(jnp.bfloat16).reshape(128, 16, 128)


def channel_sums(value):
    return jnp.sum((value[:, :128] + value[:, 128:]).T, axis=0, keepdims=True)


def start_factors(r):
    row, rep = lax.axis_index("row"), lax.axis_index("rep")
    over_rows(front_row, r)
    r.send_f[:, 0] = to_tiles(r.rows_a)
    r.send_f[:, 1] = to_tiles(r.rows_b)
    place = r.recv_f.at[row // 64, :, rep * 64 + row % 64]
    send_to_owners(r.send_f, place, r.sem.at[0], r.sem.at[1])


def own_product(r):
    x, y, z, core = coordinates()
    row, rep = lax.axis_index("row"), lax.axis_index("rep")
    wait_for(r.recv_f.at[core], r.sem.at[1])
    mine = r.recv_f.at[core, 1]
    swap = remote(mine, mine, r.sem.at[2], r.sem.at[3], (row + 1 - 2 * core, rep))
    swap.start()

    def build(half, k):
        rows = pl.ds(aligned(half * 512, 512), 512)
        slots = pl.ds(aligned(k * 64, 64), 64)
        r.right[k, rows] = unpack(r.recv_f[half, 1, slots]).astype(jnp.bfloat16)

    def own(k, carry):
        r.left[k] = unpack(r.recv_f[core, 0, pl.ds(aligned(k * 64, 64), 64)]).astype(jnp.bfloat16)
        build(core, k)
        return carry

    def other(k, carry):
        build(1 - core, k)
        return carry

    lax.fori_loop(0, 4, own, 0)
    swap.wait_recv()
    lax.fori_loop(0, 4, other, 0)

    def result(q, carry):
        part = turn(q, 1 - 2 * (x // 2), rep)
        rows = pl.ds(aligned(part * 256, 256), 256)
        total = dot(r.left[0], r.right[0, rows], NT)
        for k in range(1, 4):
            total += dot(r.left[k], r.right[k, rows], NT)
        r.back_p[:, pl.ds(aligned(part * 32, 32), 32)] = pack(total)
        start_hop(r.back_p, r.stage_p, part, r.sem.at[4], r.hop_p)
        return carry

    lax.fori_loop(0, 4, result, 0)
    swap.wait_send()
    left_swap(r).start()


def left_swap(r):
    row, rep = lax.axis_index("row"), lax.axis_index("rep")
    return remote(r.left, r.left_other, r.sem.at[5], r.sem.at[6], (row + 1 - 2 * (row % 2), rep))


def own_gradients(r):
    x, y, z, core = coordinates()
    row, rep = lax.axis_index("row"), lax.axis_index("rep")
    wait_for(r.recv_d, r.sem.at[8])
    crossing = remote(
        r.recv_d.at[pl.ds(aligned((1 - core) * 128, 128), 128)],
        r.cross, r.sem.at[9], r.sem.at[10], (row + 1 - 2 * core, rep),
    )
    crossing.start()

    def build(k, carry):
        r.d_own[k] = unpack(r.recv_d[pl.ds(aligned(k * 64, 64), 64)]).astype(jnp.bfloat16)
        return carry

    lax.fori_loop(0, 4, build, 0)
    for a in range(2):
        slots = pl.ds(aligned(core * 128 + a * 64, 64), 64)
        r.d_mine[a] = unpack(r.recv_d[slots]).T.astype(jnp.bfloat16)

    def for_left(part, carry):
        total = dot(r.d_own[0], r.right[part, pl.ds(0, 256)], NN)
        for k in range(1, 4):
            total += dot(r.d_own[k], r.right[part, pl.ds(k * 256, 256)], NN)
        r.back_d[:, pl.ds(aligned(part * 32, 32), 32), 0] = pack(total)
        return carry

    lax.fori_loop(0, 4, for_left, 0)
    crossing.wait_recv()
    for a in range(2):
        r.d_cross[a] = unpack(r.cross[pl.ds(a * 64, 64)]).T.astype(jnp.bfloat16)
    left_swap(r).wait()

    def for_right(q, carry):
        part = turn(q, 1 - 2 * (x // 2), rep)
        totals = [
            dot(r.d_mine[a], r.left[part], NN) + dot(r.d_cross[a], r.left_other[part], NN) for a in range(2)
        ]
        r.back_d[:, pl.ds(aligned(part * 32, 32), 32), 1] = pack(jnp.concatenate(totals, axis=0))
        start_hop(r.back_d, r.stage_d, part, r.sem.at[11], r.hop_d)
        return carry

    lax.fori_loop(0, 4, for_right, 0)
    crossing.wait_send()


def sum_over_devices(r, meanwhile):
    x, y, z, core = coordinates()
    row, rep = lax.axis_index("row"), lax.axis_index("rep")
    sibling = (row + 1 - 2 * core, rep)
    sends, recvs = r.sum_send, r.sum_recv

    def at(base, start, size):
        return base.at[pl.ds(aligned(start, 8), size)]

    first = remote(at(r.part, (1 - core) * 512, 512), r.from_core, sends.at[0], recvs.at[0], sibling)
    first.start()
    first.wait_recv()
    r.half[...] = r.part[pl.ds(aligned(core * 512, 512), 512)] + r.from_core[...]

    r.from_z[z] = r.half[pl.ds(aligned(z * 64, 64), 64)]
    for dz in range(1, NZ):
        tz = (z + dz) % NZ
        remote(
            at(r.half, tz * 64, 64), r.from_z.at[z], sends.at[1], recvs.at[1], device_at(x, y, tz, core)
        ).start()
    meanwhile()
    wait_for(r.from_z.at[pl.ds(0, NZ - 1)], recvs.at[1])
    r.z_sum[...] = jnp.sum(r.from_z[...], axis=0)

    r.from_xy[x * NY + y] = r.z_sum[pl.ds(aligned(y * 8, 8), 8)]
    for d in range(1, NX * NY):
        tx, ty = (x + d // NY) % NX, (y + d % NY) % NY
        remote(
            at(r.z_sum, ty * 8, 8), r.from_xy.at[x * NY + y], sends.at[2], recvs.at[2], device_at(tx, ty, z, core)
        ).start()
    wait_for(r.from_xy.at[pl.ds(0, NX * NY - 1)], recvs.at[2])
    r.xy_sum[...] = jnp.sum(r.from_xy[...], axis=0)

    r.y_rows[y] = r.xy_sum[...]
    for dy in range(1, NY):
        remote(
            r.xy_sum, r.y_rows.at[y], sends.at[3], recvs.at[3], device_at(x, (y + dy) % NY, z, core)
        ).start()
    wait_for(r.y_rows.at[pl.ds(0, NY - 1)], recvs.at[3])

    r.z_rows[z] = r.y_rows[...]
    for dz in range(1, NZ):
        remote(
            r.y_rows, r.z_rows.at[z], sends.at[4], recvs.at[4], device_at(x, y, (z + dz) % NZ, core)
        ).start()
    wait_for(r.z_rows.at[pl.ds(0, NZ - 1)], recvs.at[4])

    r.sums[core] = r.z_rows[...]
    last = remote(r.z_rows, r.sums.at[core], sends.at[5], recvs.at[5], sibling)
    last.start()
    last.wait()

    first.wait_send()
    wait_for(r.from_z.at[pl.ds(0, NZ - 1)], sends.at[1])
    wait_for(r.from_xy.at[pl.ds(0, NX * NY - 1)], sends.at[2])
    wait_for(r.y_rows.at[pl.ds(0, NY - 1)], sends.at[3])
    wait_for(r.z_rows.at[pl.ds(0, NZ - 1)], sends.at[4])


def step_kernel(names, *refs):
    r = types.SimpleNamespace(**dict(zip(names, refs)))
    x, y, z, core = coordinates()
    row, rep = lax.axis_index("row"), lax.axis_index("rep")
    owner = x % 2 == 0

    start_factors(r)

    def turn_cotangent(r, i):
        r.upstream[i] = r.cotangent[i].astype(jnp.float32).T

    over_rows(turn_cotangent, r)
    for name in ("part", "out_scale", "out_shift", "in_scale", "in_shift"):
        ref = getattr(r, name)
        ref[...] = jnp.zeros(ref.shape, ref.dtype)

    @pl.when(owner)
    def _():
        own_product(r)

    spread(r.stage_p, r.recv_p, r.hop_p, r.sem.at[12], r.sem.at[13])
    wait_for(r.recv_p, r.sem.at[13])

    to_f32_rows(r.rows_a, r.recv_p[...])
    over_rows(middle_row, r)
    r.send_d[...] = to_tiles(r.rows_b)
    send_to_owners(r.send_d, r.recv_d.at[rep * 64 + row % 64], r.sem.at[7], r.sem.at[8])

    def finish_update(r, i):
        r.update[i] = r.update_t[i].T.astype(jnp.bfloat16)
        r.part[pl.ds(640, 128)] += dot(r.xn[i], r.d_proj_out[i], NT)

    over_rows(finish_update, r)

    @pl.when(owner)
    def _():
        own_gradients(r)

    spread(r.stage_d, r.recv_g, r.hop_d, r.sem.at[14], r.sem.at[15])
    wait_for(r.recv_g, r.sem.at[15])

    to_f32_rows(r.rows_a, r.recv_g[:, 0])
    to_f32_rows(r.rows_b, r.recv_g[:, 1])
    over_rows(back_row, r)
    norms = [channel_sums(ref[...]) for ref in (r.in_scale, r.in_shift, r.out_scale, r.out_shift)]
    r.part[pl.ds(768, 8)] = jnp.concatenate(norms + [jnp.zeros((4, 128), jnp.float32)], axis=0)

    sum_over_devices(r, lambda: over_rows(grad_row, r))

    finish_sends(r.send_f, r.sem.at[0])
    finish_sends(r.send_d, r.sem.at[7])
    wait_for(r.stage_p.at[pl.ds(0, 127)], r.sem.at[12])
    wait_for(r.stage_d.at[pl.ds(0, 127)], r.sem.at[14])

    @pl.when(owner)
    def _():
        finish_hop(r.back_p, r.sem.at[4])
        finish_hop(r.back_d, r.sem.at[11])


VMEM = pl.BlockSpec(memory_space=pltpu.VMEM)
DMA = pltpu.SemaphoreType.DMA


def scratch():
    f32, bf16 = jnp.float32, jnp.bfloat16

    def of(dtype, *shape):
        return pltpu.VMEM(shape, dtype)

    return {
        "rows_a": of(f32, 2048, 128),
        "rows_b": of(f32, 2048, 128),
        "z_hat": of(f32, 8, 128, 256),
        "z_inv": of(f32, 8, 256),
        "normed": of(bf16, 8, 128, 256),
        "value": of(f32, 8, 2, 128, 256),
        "sig": of(f32, 8, 2, 128, 256),
        "gating": of(f32, 8, 128, 256),
        "upstream": of(f32, 8, 128, 256),
        "xn": of(bf16, 8, 128, 256),
        "update_t": of(f32, 8, 128, 256),
        "d_proj_out": of(bf16, 8, 128, 256),
        "d_proj": of(bf16, 8, 640, 256),
        "d_normed": of(f32, 8, 128, 256),
        "out_scale": of(f32, 128, 256),
        "out_shift": of(f32, 128, 256),
        "in_scale": of(f32, 128, 256),
        "in_shift": of(f32, 128, 256),
        "send_f": of(bf16, 128, 2, 16, 128),
        "recv_f": of(bf16, 2, 2, 256, 16, 128),
        "left": of(bf16, 4, 512, 256),
        "right": of(bf16, 4, 1024, 256),
        "back_p": of(bf16, 2, 128, 16, 128),
        "stage_p": of(bf16, 128, 16, 128),
        "recv_p": of(bf16, 128, 16, 128),
        "send_d": of(bf16, 128, 16, 128),
        "recv_d": of(bf16, 256, 16, 128),
        "left_other": of(bf16, 4, 512, 256),
        "cross": of(bf16, 128, 16, 128),
        "d_own": of(bf16, 4, 512, 256),
        "d_mine": of(bf16, 2, 256, 512),
        "d_cross": of(bf16, 2, 256, 512),
        "back_d": of(bf16, 2, 128, 2, 16, 128),
        "stage_d": of(bf16, 128, 2, 16, 128),
        "recv_g": of(bf16, 128, 2, 16, 128),
        "part": of(f32, 1024, 128),
        "from_core": of(f32, 512, 128),
        "half": of(f32, 512, 128),
        "from_z": of(f32, 8, 64, 128),
        "z_sum": of(f32, 64, 128),
        "from_xy": of(f32, 32, 8, 128),
        "xy_sum": of(f32, 8, 128),
        "y_rows": of(f32, 8, 8, 128),
        "z_rows": of(f32, 8, 8, 8, 128),
        "sem": DMA((16,)),
        "hop_p": DMA((4,)),
        "hop_d": DMA((4,)),
        "sum_send": DMA((6,)),
        "sum_recv": DMA((6,)),
    }


INPUTS = (
    "pair", "cotangent", "mask", "in_gain", "in_bias", "out_gain", "out_bias", "proj_w", "proj_t", "out_w", "out_t",
)
OUTPUTS = ("update", "grad_pair", "sums")


def whole_step(*args):
    extra = scratch()
    names = INPUTS + OUTPUTS + tuple(extra)
    block = jax.ShapeDtypeStruct((8, 256, 128), jnp.bfloat16)
    return pl.pallas_call(
        functools.partial(step_kernel, names),
        out_shape=(block, block, jax.ShapeDtypeStruct((2, 8, 8, 8, 128), jnp.float32)),
        in_specs=[VMEM] * len(INPUTS),
        out_specs=(VMEM,) * 3,
        scratch_shapes=list(extra.values()),
        compiler_params=pltpu.CompilerParams(has_side_effects=True, vmem_limit_bytes=56 << 20),
        name="triangle_step",
    )(*args)


def body(
    pair, cotangent, token_mask, in_gain, in_bias, proj_weight, out_gain, out_bias, out_weight
):
    row_count, col_count, channels = pair.shape
    mask_f = token_mask.astype(jnp.float32)
    rows = lax.dynamic_slice_in_dim(mask_f, lax.axis_index("row") * row_count, row_count)
    cols = lax.dynamic_slice_in_dim(mask_f, lax.axis_index("rep") * col_count, col_count)
    vectors = [
        jnp.broadcast_to(v[:, None], (channels, 128)) for v in (in_gain, in_bias, out_gain, out_bias)
    ]
    update, grad_pair, sums = whole_step(
        pair, cotangent, rows[:, None] * cols[None, :], *vectors,
        proj_weight, proj_weight.T, out_weight, out_weight.T,
    )
    total = sums.reshape(1024, 128) * (1.0 / token_mask.shape[0])
    return (update, grad_pair, total[:640].T, total[640:768], total[768:770], total[770:772])


def solution(mesh):
    in_specs = (P("row", "rep", None), P("row", "rep", None), P(), P(), P(), P(), P(), P(), P())
    out_specs = (P("row", "rep", None), P("row", "rep", None), P(), P(), P(), P())
    return jax.shard_map(body, mesh=mesh, in_specs=in_specs, out_specs=out_specs, check_vma=False)
```

```python
import functools
import types

import jax
import jax.numpy as jnp
from jax import lax
from jax.experimental import pallas as pl
from jax.experimental.pallas import tpu as pltpu
from jax.sharding import PartitionSpec as P

EPSILON = 1e-05
MESH = pl.DeviceIdType.MESH
NX, NY, NZ = 4, 8, 8


def coordinates():
    row, rep = lax.axis_index("row"), lax.axis_index("rep")
    return row // 32, rep * 2 + (row // 16) % 2, (row // 2) % 8, row % 2


def device_at(x, y, z, core):
    return (((x * 2 + y % 2) * 8 + z) * 2 + core, y // 2)


def remote(src, dst, send_sem, recv_sem, target):
    return pltpu.make_async_remote_copy(
        src, dst, send_sem, recv_sem, device_id=target, device_id_type=MESH
    )


def copy_to(src, dst, send_sem, recv_sem, target, me):
    same = jnp.logical_and(target[0] == me[0], target[1] == me[1])

    @pl.when(same)
    def _():
        pltpu.make_async_copy(src, dst, recv_sem).start()

    @pl.when(jnp.logical_not(same))
    def _():
        remote(src, dst, send_sem, recv_sem, target).start()


def wait_for(ref, sem):
    pltpu.make_async_copy(ref, ref, sem).wait()


def send_to_owners(send, place, send_sem, recv_sem, first=0, last=128):
    x, y, z, core = coordinates()
    me = (lax.axis_index("row"), lax.axis_index("rep"))
    sign = 1 - 2 * core

    def step(s, carry):
        dz, dy, dx = s % 8, (s // 8) % 8, s // 64
        hx = (x // 2 + dx) % 2
        ty, tz = (y + sign * dy + 8) % 8, (z + sign * dz + 8) % 8
        h = hx * 64 + ty * 8 + tz
        copy_to(send.at[h], place, send_sem, recv_sem, device_at(2 * hx, ty, tz, x // 2), me)
        return carry

    lax.fori_loop(first, last, step, 0)


def finish_sends(send, send_sem):
    x, y, z, core = coordinates()
    keeps = jnp.logical_and(x % 2 == 0, core == x // 2)

    @pl.when(keeps)
    def _():
        wait_for(send.at[pl.ds(0, 127)], send_sem)

    @pl.when(jnp.logical_not(keeps))
    def _():
        wait_for(send, send_sem)


def aligned(start, unit):
    return pl.multiple_of(start, unit)


def unpack(slots):
    wide = slots.astype(jnp.float32)
    low, high = wide[:, :8].reshape(512, 128), wide[:, 8:].reshape(512, 128)
    return jnp.concatenate([low, high], axis=1)


def pack(block):
    low, high = block[:, :128].reshape(64, 8, 128), block[:, 128:].reshape(64, 8, 128)
    return jnp.concatenate([low, high], axis=1).astype(jnp.bfloat16).reshape(2, 32, 16, 128)


def dot(a, b, contract):
    return lax.dot_general(a, b, ((contract[0], contract[1]), ((), ())), preferred_element_type=jnp.float32)


def turn(q, sign, rep):
    return (rep + sign * q + 4) % 4


def start_hop(send, stage, part, hop_send, hop_recv):
    x, y, z, core = coordinates()
    me = (lax.axis_index("row"), lax.axis_index("rep"))
    rows = pl.ds(aligned(part * 32, 32), 32)
    for bx in range(2):
        target = device_at(2 * core + bx, y, z, x // 2)
        copy_to(send.at[bx, rows], stage.at[rows], hop_send, hop_recv.at[part], target, me)


def finish_hop(send, hop_send):
    x, y, z, core = coordinates()

    @pl.when(core == x // 2)
    def _():
        wait_for(send.at[0], hop_send)

    @pl.when(core != x // 2)
    def _():
        wait_for(send, hop_send)


def spread(stage, recv, hop_recv, send_sem, recv_sem):
    x, y, z, core = coordinates()
    rep = lax.axis_index("rep")
    me = (lax.axis_index("row"), rep)
    h = core * 64 + y * 8 + z
    sign = 1 - 2 * core

    def one_part(q, carry):
        part = turn(q, sign, rep)
        wait_for(stage.at[pl.ds(aligned(part * 32, 32), 32)], hop_recv.at[part])

        def step(s, carry):
            tc, dz, dy = (s + core) % 2, (s // 2) % 8, s // 16
            ty, tz = part * 2 + (y + dy) % 2, (z + sign * dz + 8) % 8
            place = part * 32 + (ty % 2) * 16 + tz * 2 + tc
            copy_to(stage.at[place], recv.at[h], send_sem, recv_sem, device_at(x, ty, tz, tc), me)
            return carry

        lax.fori_loop(0, 32, step, 0)
        return carry

    lax.fori_loop(0, 4, one_part, 0)


def rows_of(ref, row):
    return ref[pl.ds(row, 128, stride=16), :]


def load_row(ref, i):
    return jnp.concatenate([rows_of(ref, i), rows_of(ref, 8 + i)], axis=1)


def store_row(ref, i, value):
    ref[pl.ds(i, 128, stride=16), :] = value[:, :128]
    ref[pl.ds(8 + i, 128, stride=16), :] = value[:, 128:]


def mean0(value):
    return jnp.sum(value, axis=0, keepdims=True) * (1.0 / value.shape[0])


def standardize(value):
    centred = value - mean0(value)
    inv_std = lax.rsqrt(mean0(centred * centred) + EPSILON)
    return centred * inv_std, inv_std


def standardize_back(scaled, normed, inv_std):
    return inv_std * (scaled - mean0(scaled) - normed * mean0(scaled * normed))


def wide(column):
    return jnp.concatenate([column, column], axis=1)


NN, NT = ((1,), (0,)), ((1,), (1,))


def neighbours():
    x, y, z, core = coordinates()
    in_z = [device_at(x, y, (z + d // 2) % NZ, (core + d) % 2) for d in range(1, 2 * NZ)]
    in_y = [device_at(x, (y + d) % NY, z, core) for d in range(1, NY)]
    in_x = [device_at((x + d) % NX, y, z, core) for d in range(1, NX)]
    return in_z, in_y, in_x


def greet(targets, sem):
    for target in targets:
        pl.semaphore_signal(sem, inc=1, device_id=target, device_id_type=MESH)


def front_row(r, i):
    z_hat, z_inv = standardize(r.pair[i].astype(jnp.float32).T)
    r.z_hat[i] = z_hat
    r.z_inv[pl.ds(i, 1)] = z_inv
    normed = (z_hat * wide(r.in_gain[...]) + wide(r.in_bias[...])).astype(jnp.bfloat16)
    r.normed[i] = normed
    proj = dot(r.proj_t[...], normed, NN)
    mask = r.mask[pl.ds(i, 1)]
    for t, rows in ((0, r.rows_a), (1, r.rows_b)):
        value, gate = proj[t * 256 : t * 256 + 128], proj[t * 256 + 128 : t * 256 + 256]
        sig = jax.nn.sigmoid(gate)
        r.value[i, t] = value
        r.sig[i, t] = sig
        store_row(rows, i, mask * sig * value)
    r.gating[i] = jax.nn.sigmoid(proj[512:])


def middle_row(r, i):
    x_hat, x_inv = standardize(load_row(r.rows_a, i))
    gain = wide(r.out_gain[...])
    xn = (x_hat * gain + wide(r.out_bias[...])).astype(jnp.bfloat16)
    r.xn[i] = xn
    projected = dot(r.out_t[...], xn, NN)
    gating, upstream = r.gating[i], r.upstream[i]
    r.update_t[i] = gating * projected
    d_proj_out = (upstream * gating).astype(jnp.bfloat16)
    r.d_proj_out[i] = d_proj_out
    r.d_gate[i] = (upstream * projected * gating * (1.0 - gating)).astype(jnp.bfloat16)
    d_xn = dot(r.out_w[...], d_proj_out, NN)
    r.out_scale[...] += d_xn * x_hat
    r.out_shift[...] += d_xn
    store_row(r.rows_b, i, standardize_back(d_xn * gain, x_hat, x_inv))


def back_row(r, i, t, rows):
    d_factor = load_row(rows, i) * r.mask[pl.ds(i, 1)]
    value, sig = r.value[i, t], r.sig[i, t]
    d_value = (d_factor * sig).astype(jnp.bfloat16)
    d_gate = (d_factor * value * sig * (1.0 - sig)).astype(jnp.bfloat16)
    d_proj = jnp.concatenate([d_value, d_gate], axis=0)
    r.part[pl.ds(t * 256, 256)] += dot(d_proj, r.normed[i], NT)
    return r.d_normed[i] + dot(r.proj_w[:, t * 256 : t * 256 + 256], d_proj, NN)


def left_row(r, i):
    r.d_normed[i] = back_row(r, i, 0, r.rows_a)


def right_row(r, i):
    d_normed = back_row(r, i, 1, r.rows_b)
    r.d_normed[i] = d_normed
    r.in_scale[...] += d_normed * r.z_hat[i]
    r.in_shift[...] += d_normed


def grad_row(r, i):
    scaled = r.d_normed[i] * wide(r.in_gain[...])
    result = standardize_back(scaled, r.z_hat[i], r.z_inv[pl.ds(i, 1)])
    r.grad_pair[i] = result.T.astype(jnp.bfloat16)


def over_rows(function, r):
    def step(i, carry):
        function(r, i)
        return carry

    lax.fori_loop(0, 8, step, 0)


def to_f32_rows(rows, tiles):
    rows[...] = tiles.astype(jnp.float32).reshape(2048, 128)


def to_tiles(rows):
    return rows[...].astype(jnp.bfloat16).reshape(128, 16, 128)


def channel_sums(value):
    return jnp.sum((value[:, :128] + value[:, 128:]).T, axis=0, keepdims=True)


def prepare(r):
    row, rep = lax.axis_index("row"), lax.axis_index("rep")
    r.proj_t[...] = r.proj_w[...].astype(jnp.float32).T.astype(jnp.bfloat16)
    r.out_t[...] = r.out_w[...].astype(jnp.float32).T.astype(jnp.bfloat16)
    for column, vector in (
        (r.in_gain, r.in_gain_row), (r.in_bias, r.in_bias_row), (r.out_gain, r.out_gain_row), (r.out_bias, r.out_bias_row),
    ):
        column[...] = jnp.broadcast_to(vector[...], (128, 128)).T
    cols = jnp.concatenate([r.mask_cols[pl.ds(rep * 2, 1)], r.mask_cols[pl.ds(rep * 2 + 1, 1)]], axis=1)
    cols = cols.astype(jnp.float32)
    for i in range(8):
        r.mask[pl.ds(i, 1)] = cols * r.mask_rows[row * 8 + i].astype(jnp.float32)


def enter(r):
    in_z, in_y, in_x = neighbours()
    barrier = pltpu.get_barrier_semaphore()
    greet(in_z + in_y + in_x, barrier)
    prepare(r)

    def step(i, carry):
        front_row(r, i)
        return carry

    lax.fori_loop(0, 4, step, 0)
    pl.semaphore_wait(barrier, len(in_z) + len(in_y) + len(in_x))
    greet(in_y, r.plane_sem)
    lax.fori_loop(4, 8, step, 0)
    pl.semaphore_wait(r.plane_sem, len(in_y))
    greet(in_x, r.all_sem)
    r.send_r[...] = to_tiles(r.rows_b)
    r.send_l[...] = to_tiles(r.rows_a)
    pl.semaphore_wait(r.all_sem, len(in_x))


def swap_right(r):
    row, rep = lax.axis_index("row"), lax.axis_index("rep")
    mine = r.recv_r.at[row % 2]
    return remote(mine, mine, r.sem.at[2], r.sem.at[3], (row + 1 - 2 * (row % 2), rep))


def send_factors(r):
    row, rep = lax.axis_index("row"), lax.axis_index("rep")
    half, slot = row // 64, rep * 64 + row % 64
    send_to_owners(r.send_r, r.recv_r.at[half, slot], r.sem.at[0], r.sem.at[1])
    send_to_owners(r.send_l, r.recv_l.at[slot], r.sem.at[16], r.sem.at[17], 0, 32)

    @pl.when((row // 32) % 2 == 0)
    def _():
        wait_for(r.recv_r.at[row % 2], r.sem.at[1])
        swap_right(r).start()

    send_to_owners(r.send_l, r.recv_l.at[slot], r.sem.at[16], r.sem.at[17], 32, 128)


def own_product(r):
    x, y, z, core = coordinates()
    rep = lax.axis_index("rep")

    def build(half):
        def step(k, carry):
            rows = pl.ds(aligned(half * 512, 512), 512)
            slots = pl.ds(aligned(k * 64, 64), 64)
            r.right[k, rows] = unpack(r.recv_r[half, slots]).astype(jnp.bfloat16)
            return carry

        lax.fori_loop(0, 4, step, 0)

    def build_left(k, carry):
        r.left[k] = unpack(r.recv_l[pl.ds(aligned(k * 64, 64), 64)]).astype(jnp.bfloat16)
        return carry

    build(core)
    swap_right(r).wait()
    build(1 - core)
    wait_for(r.recv_l, r.sem.at[17])
    lax.fori_loop(0, 4, build_left, 0)

    def result(q, carry):
        part = turn(q, 1 - 2 * (x // 2), rep)
        rows = pl.ds(aligned(part * 256, 256), 256)
        total = dot(r.left[0], r.right[0, rows], NT)
        for k in range(1, 4):
            total += dot(r.left[k], r.right[k, rows], NT)
        r.back_p[:, pl.ds(aligned(part * 32, 32), 32)] = pack(total)
        start_hop(r.back_p, r.stage_p, part, r.sem.at[4], r.hop_p)
        return carry

    lax.fori_loop(0, 4, result, 0)
    left_swap(r).start()


def left_swap(r):
    row, rep = lax.axis_index("row"), lax.axis_index("rep")
    return remote(r.left, r.left_other, r.sem.at[5], r.sem.at[6], (row + 1 - 2 * (row % 2), rep))


def own_gradients(r):
    x, y, z, core = coordinates()
    row, rep = lax.axis_index("row"), lax.axis_index("rep")
    wait_for(r.recv_d, r.sem.at[8])
    crossing = remote(
        r.recv_d.at[pl.ds(aligned((1 - core) * 128, 128), 128)],
        r.cross, r.sem.at[9], r.sem.at[10], (row + 1 - 2 * core, rep),
    )
    crossing.start()

    def build(k, carry):
        r.d_own[k] = unpack(r.recv_d[pl.ds(aligned(k * 64, 64), 64)]).astype(jnp.bfloat16)
        return carry

    lax.fori_loop(0, 4, build, 0)
    def for_left(q, carry):
        part = turn(q, 1 - 2 * (x // 2), rep)
        total = dot(r.d_own[0], r.right[part, pl.ds(0, 256)], NN)
        for k in range(1, 4):
            total += dot(r.d_own[k], r.right[part, pl.ds(k * 256, 256)], NN)
        r.back_l[:, pl.ds(aligned(part * 32, 32), 32)] = pack(total)
        start_hop(r.back_l, r.stage_l, part, r.sem.at[11], r.hop_l)
        return carry

    lax.fori_loop(0, 4, for_left, 0)
    for a in range(2):
        slots = pl.ds(aligned(core * 128 + a * 64, 64), 64)
        r.d_mine[a] = unpack(r.recv_d[slots]).T.astype(jnp.bfloat16)
    crossing.wait()
    for a in range(2):
        r.d_cross[a] = unpack(r.cross[pl.ds(a * 64, 64)]).T.astype(jnp.bfloat16)
    left_swap(r).wait()

    def for_right(q, carry):
        part = turn(q, 1 - 2 * (x // 2), rep)
        totals = [
            dot(r.d_mine[a], r.left[part], NN) + dot(r.d_cross[a], r.left_other[part], NN) for a in range(2)
        ]
        r.back_r[:, pl.ds(aligned(part * 32, 32), 32)] = pack(jnp.concatenate(totals, axis=0))
        start_hop(r.back_r, r.stage_r, part, r.sem.at[18], r.hop_r)
        return carry

    lax.fori_loop(0, 4, for_right, 0)


def sum_over_devices(r, meanwhile):
    x, y, z, core = coordinates()
    row, rep = lax.axis_index("row"), lax.axis_index("rep")
    sibling = (row + 1 - 2 * core, rep)
    sends, recvs = r.sum_send, r.sum_recv

    def at(base, start, size):
        return base.at[pl.ds(aligned(start, 8), size)]

    first = remote(at(r.part, (1 - core) * 512, 512), r.from_core, sends.at[0], recvs.at[0], sibling)
    first.start()
    first.wait_recv()
    r.half[...] = r.part[pl.ds(aligned(core * 512, 512), 512)] + r.from_core[...]

    r.from_z[z] = r.half[pl.ds(aligned(z * 64, 64), 64)]
    for dz in range(1, NZ):
        tz = (z + dz) % NZ
        remote(
            at(r.half, tz * 64, 64), r.from_z.at[z], sends.at[1], recvs.at[1], device_at(x, y, tz, core)
        ).start()
    meanwhile()
    wait_for(r.from_z.at[pl.ds(0, NZ - 1)], recvs.at[1])
    r.z_sum[...] = jnp.sum(r.from_z[...], axis=0)

    r.from_xy[x * NY + y] = r.z_sum[pl.ds(aligned(y * 8, 8), 8)]
    for d in range(1, NX * NY):
        tx, ty = (x + d // NY) % NX, (y + d % NY) % NY
        remote(
            at(r.z_sum, ty * 8, 8), r.from_xy.at[x * NY + y], sends.at[2], recvs.at[2], device_at(tx, ty, z, core)
        ).start()
    wait_for(r.from_xy.at[pl.ds(0, NX * NY - 1)], recvs.at[2])
    r.xy_sum[...] = jnp.sum(r.from_xy[...], axis=0)

    r.y_rows[y] = r.xy_sum[...]
    for dy in range(1, NY):
        remote(
            r.xy_sum, r.y_rows.at[y], sends.at[3], recvs.at[3], device_at(x, (y + dy) % NY, z, core)
        ).start()
    wait_for(r.y_rows.at[pl.ds(0, NY - 1)], recvs.at[3])

    r.z_part[...] = r.y_rows[...].reshape(64, 128).astype(jnp.bfloat16)
    r.z_rows[z] = r.z_part[...]
    for dz in range(1, NZ):
        remote(
            r.z_part, r.z_rows.at[z], sends.at[4], recvs.at[4], device_at(x, y, (z + dz) % NZ, core)
        ).start()
    wait_for(r.z_rows.at[pl.ds(0, NZ - 1)], recvs.at[4])

    r.both[core] = r.z_rows[...]
    last = remote(r.z_rows, r.both.at[core], sends.at[5], recvs.at[5], sibling)
    last.start()
    last.wait()
    r.sums[...] = r.both[...].reshape(1024, 128).astype(jnp.float32) * (1.0 / r.mask_rows.shape[0])

    first.wait_send()
    wait_for(r.from_z.at[pl.ds(0, NZ - 1)], sends.at[1])
    wait_for(r.from_xy.at[pl.ds(0, NX * NY - 1)], sends.at[2])
    wait_for(r.y_rows.at[pl.ds(0, NY - 1)], sends.at[3])
    wait_for(r.z_rows.at[pl.ds(0, NZ - 1)], sends.at[4])


def step_kernel(names, *refs):
    r = types.SimpleNamespace(**dict(zip(names, refs)))
    x, y, z, core = coordinates()
    row, rep = lax.axis_index("row"), lax.axis_index("rep")
    owner = x % 2 == 0

    enter(r)
    send_factors(r)

    def turn_cotangent(r, i):
        r.upstream[i] = r.cotangent[i].astype(jnp.float32).T

    over_rows(turn_cotangent, r)
    for name in ("part", "out_scale", "out_shift", "in_scale", "in_shift"):
        ref = getattr(r, name)
        ref[...] = jnp.zeros(ref.shape, ref.dtype)

    @pl.when(owner)
    def _():
        own_product(r)

    spread(r.stage_p, r.recv_p, r.hop_p, r.sem.at[12], r.sem.at[13])
    wait_for(r.recv_p, r.sem.at[13])

    to_f32_rows(r.rows_a, r.recv_p[...])
    over_rows(middle_row, r)
    r.send_d[...] = to_tiles(r.rows_b)
    send_to_owners(r.send_d, r.recv_d.at[rep * 64 + row % 64], r.sem.at[7], r.sem.at[8])

    def finish_middle(r, i):
        r.update[i] = r.update_t[i].T.astype(jnp.bfloat16)
        d_gate = r.d_gate[i]
        r.part[pl.ds(512, 128)] += dot(d_gate, r.normed[i], NT)
        r.part[pl.ds(640, 128)] += dot(r.xn[i], r.d_proj_out[i], NT)
        r.d_normed[i] = dot(r.proj_w[:, 512:], d_gate, NN)

    over_rows(finish_middle, r)

    @pl.when(owner)
    def _():
        own_gradients(r)

    spread(r.stage_l, r.recv_gl, r.hop_l, r.sem.at[14], r.sem.at[15])
    spread(r.stage_r, r.recv_gr, r.hop_r, r.sem.at[19], r.sem.at[20])
    wait_for(r.recv_gl, r.sem.at[15])
    to_f32_rows(r.rows_a, r.recv_gl[...])
    over_rows(left_row, r)
    wait_for(r.recv_gr, r.sem.at[20])
    to_f32_rows(r.rows_b, r.recv_gr[...])
    over_rows(right_row, r)
    norms = [channel_sums(ref[...]) for ref in (r.in_scale, r.in_shift, r.out_scale, r.out_shift)]
    r.part[pl.ds(768, 8)] = jnp.concatenate(norms + [jnp.zeros((4, 128), jnp.float32)], axis=0)

    sum_over_devices(r, lambda: over_rows(grad_row, r))

    finish_sends(r.send_r, r.sem.at[0])
    finish_sends(r.send_l, r.sem.at[16])
    finish_sends(r.send_d, r.sem.at[7])
    wait_for(r.stage_p.at[pl.ds(0, 127)], r.sem.at[12])
    wait_for(r.stage_l.at[pl.ds(0, 127)], r.sem.at[14])
    wait_for(r.stage_r.at[pl.ds(0, 127)], r.sem.at[19])

    @pl.when(owner)
    def _():
        finish_hop(r.back_p, r.sem.at[4])
        finish_hop(r.back_l, r.sem.at[11])
        finish_hop(r.back_r, r.sem.at[18])


VMEM = pl.BlockSpec(memory_space=pltpu.VMEM)
DMA = pltpu.SemaphoreType.DMA


def scratch():
    f32, bf16 = jnp.float32, jnp.bfloat16

    def of(dtype, *shape):
        return pltpu.VMEM(shape, dtype)

    return {
        "rows_a": of(f32, 2048, 128),
        "rows_b": of(f32, 2048, 128),
        "z_hat": of(f32, 8, 128, 256),
        "z_inv": of(f32, 8, 256),
        "normed": of(bf16, 8, 128, 256),
        "value": of(f32, 8, 2, 128, 256),
        "sig": of(f32, 8, 2, 128, 256),
        "gating": of(f32, 8, 128, 256),
        "upstream": of(f32, 8, 128, 256),
        "xn": of(bf16, 8, 128, 256),
        "update_t": of(f32, 8, 128, 256),
        "d_proj_out": of(bf16, 8, 128, 256),
        "d_gate": of(bf16, 8, 128, 256),
        "mask": of(f32, 8, 256),
        "in_gain": of(f32, 128, 128),
        "in_bias": of(f32, 128, 128),
        "out_gain": of(f32, 128, 128),
        "out_bias": of(f32, 128, 128),
        "proj_t": of(bf16, 640, 128),
        "out_t": of(bf16, 128, 128),
        "d_normed": of(f32, 8, 128, 256),
        "out_scale": of(f32, 128, 256),
        "out_shift": of(f32, 128, 256),
        "in_scale": of(f32, 128, 256),
        "in_shift": of(f32, 128, 256),
        "send_l": of(bf16, 128, 16, 128),
        "send_r": of(bf16, 128, 16, 128),
        "recv_l": of(bf16, 256, 16, 128),
        "recv_r": of(bf16, 2, 256, 16, 128),
        "left": of(bf16, 4, 512, 256),
        "right": of(bf16, 4, 1024, 256),
        "back_p": of(bf16, 2, 128, 16, 128),
        "stage_p": of(bf16, 128, 16, 128),
        "recv_p": of(bf16, 128, 16, 128),
        "send_d": of(bf16, 128, 16, 128),
        "recv_d": of(bf16, 256, 16, 128),
        "left_other": of(bf16, 4, 512, 256),
        "cross": of(bf16, 128, 16, 128),
        "d_own": of(bf16, 4, 512, 256),
        "d_mine": of(bf16, 2, 256, 512),
        "d_cross": of(bf16, 2, 256, 512),
        "back_l": of(bf16, 2, 128, 16, 128),
        "back_r": of(bf16, 2, 128, 16, 128),
        "stage_l": of(bf16, 128, 16, 128),
        "stage_r": of(bf16, 128, 16, 128),
        "recv_gl": of(bf16, 128, 16, 128),
        "recv_gr": of(bf16, 128, 16, 128),
        "part": of(f32, 1024, 128),
        "from_core": of(f32, 512, 128),
        "half": of(f32, 512, 128),
        "from_z": of(f32, 8, 64, 128),
        "z_sum": of(f32, 64, 128),
        "from_xy": of(f32, 32, 8, 128),
        "xy_sum": of(f32, 8, 128),
        "y_rows": of(f32, 8, 8, 128),
        "z_part": of(bf16, 64, 128),
        "z_rows": of(bf16, 8, 64, 128),
        "both": of(bf16, 2, 8, 64, 128),
        "sem": DMA((21,)),
        "hop_p": DMA((4,)),
        "hop_l": DMA((4,)),
        "hop_r": DMA((4,)),
        "plane_sem": pltpu.SemaphoreType.REGULAR,
        "all_sem": pltpu.SemaphoreType.REGULAR,
        "sum_send": DMA((6,)),
        "sum_recv": DMA((6,)),
    }


INPUTS = (
    "mask_rows", "mask_cols", "pair", "cotangent", "in_gain_row", "in_bias_row", "out_gain_row", "out_bias_row",
    "proj_w", "out_w",
)
OUTPUTS = ("update", "grad_pair", "sums")


def whole_step(*args):
    extra = scratch()
    names = INPUTS + OUTPUTS + tuple(extra)
    block = jax.ShapeDtypeStruct((8, 256, 128), jnp.bfloat16)
    return pl.pallas_call(
        functools.partial(step_kernel, names),
        out_shape=(block, block, jax.ShapeDtypeStruct((1024, 128), jnp.float32)),
        in_specs=[pl.BlockSpec(memory_space=pltpu.SMEM)] + [VMEM] * (len(INPUTS) - 1),
        out_specs=(VMEM,) * 3,
        scratch_shapes=list(extra.values()),
        compiler_params=pltpu.CompilerParams(
            has_side_effects=True, collective_id=0, vmem_limit_bytes=56 << 20
        ),
        name="triangle_step",
    )(*args)


def body(
    pair, cotangent, token_mask, in_gain, in_bias, proj_weight, out_gain, out_bias, out_weight
):
    update, grad_pair, total = whole_step(
        token_mask,
        token_mask.reshape(8, 128),
        pair,
        cotangent,
        *[v.reshape(1, 128) for v in (in_gain, in_bias, out_gain, out_bias)],
        proj_weight,
        out_weight,
    )
    return (update, grad_pair, total[:640].T, total[640:768], total[768:770], total[770:772])


def solution(mesh):
    in_specs = (P("row", "rep", None), P("row", "rep", None), P(), P(), P(), P(), P(), P(), P())
    out_specs = (P("row", "rep", None), P("row", "rep", None), P(), P(), P(), P())
    return jax.shard_map(body, mesh=mesh, in_specs=in_specs, out_specs=out_specs, check_vma=False)
```

```python
import functools
import types

import jax
import jax.numpy as jnp
from jax import lax
from jax.experimental import pallas as pl
from jax.experimental.pallas import tpu as pltpu
from jax.sharding import PartitionSpec as P

EPSILON = 1e-05
MESH = pl.DeviceIdType.MESH
NX, NY, NZ = 4, 8, 8


def coordinates():
    row, rep = lax.axis_index("row"), lax.axis_index("rep")
    return row // 32, rep * 2 + (row // 16) % 2, (row // 2) % 8, row % 2


def device_at(x, y, z, core):
    return (((x * 2 + y % 2) * 8 + z) * 2 + core, y // 2)


def remote(src, dst, send_sem, recv_sem, target):
    return pltpu.make_async_remote_copy(
        src, dst, send_sem, recv_sem, device_id=target, device_id_type=MESH
    )


def copy_to(src, dst, send_sem, recv_sem, target, me):
    same = jnp.logical_and(target[0] == me[0], target[1] == me[1])

    @pl.when(same)
    def _():
        pltpu.make_async_copy(src, dst, recv_sem).start()

    @pl.when(jnp.logical_not(same))
    def _():
        remote(src, dst, send_sem, recv_sem, target).start()


def wait_for(ref, sem):
    pltpu.make_async_copy(ref, ref, sem).wait()


def send_to_owners(send, place, send_sem, recv_sem, first=0, last=128):
    x, y, z, core = coordinates()
    me = (lax.axis_index("row"), lax.axis_index("rep"))
    sign = 1 - 2 * core

    def step(s, carry):
        dz, dy, dx = s % 8, (s // 8) % 8, s // 64
        hx = (x // 2 + dx) % 2
        ty, tz = (y + sign * dy + 8) % 8, (z + sign * dz + 8) % 8
        h = hx * 64 + ty * 8 + tz
        copy_to(send.at[h], place, send_sem, recv_sem, device_at(2 * hx, ty, tz, x // 2), me)
        return carry

    lax.fori_loop(first, last, step, 0)


def finish_sends(send, send_sem):
    x, y, z, core = coordinates()
    keeps = jnp.logical_and(x % 2 == 0, core == x // 2)

    @pl.when(keeps)
    def _():
        wait_for(send.at[pl.ds(0, 127)], send_sem)

    @pl.when(jnp.logical_not(keeps))
    def _():
        wait_for(send, send_sem)


def aligned(start, unit):
    return pl.multiple_of(start, unit)


def unpack(slots):
    wide = slots.astype(jnp.float32)
    low, high = wide[:, :8].reshape(512, 128), wide[:, 8:].reshape(512, 128)
    return jnp.concatenate([low, high], axis=1)


def pack(block):
    low, high = block[:, :128].reshape(64, 8, 128), block[:, 128:].reshape(64, 8, 128)
    return jnp.concatenate([low, high], axis=1).astype(jnp.bfloat16).reshape(2, 32, 16, 128)


def dot(a, b, contract):
    return lax.dot_general(a, b, ((contract[0], contract[1]), ((), ())), preferred_element_type=jnp.float32)


def turn(q, sign, rep):
    return (rep + sign * q + 4) % 4


def way_back():
    x, y, z, core = coordinates()
    even = x % 2 == 0
    hx = jnp.where(even, x // 2, core)
    half = jnp.where(even, core, x // 2)
    differ = (hx + half) % 2
    plane = jnp.where(even, (x + 3 * differ) % 4, 2 * half + 1 - differ)
    return hx, half, differ, plane


def start_hop(send, stage, part, hop_send, hop_recv):
    x, y, z, core = coordinates()
    hx, half, differ, plane = way_back()
    rows = pl.ds(aligned(part * 32, 32), 32)
    target = device_at((x + 1 + 2 * differ) % 4, y, z, hx)
    other = 1 - (plane - 2 * half)
    remote(send.at[other, rows], stage.at[rows], hop_send, hop_recv.at[part], target).start()


def finish_hop(send, hop_send):
    wait_for(send.at[0], hop_send)


def spread(send, stage, recv, hop_recv, send_sem, recv_sem):
    x, y, z, core = coordinates()
    rep = lax.axis_index("rep")
    me = (lax.axis_index("row"), rep)
    hx, half, differ, plane = way_back()
    h = hx * 64 + y * 8 + z
    sign = 1 - 2 * core

    def all_parts(source, staged):
        def one_part(q, carry):
            part = turn(q, 1 - 2 * differ, rep)
            if staged:
                wait_for(source.at[pl.ds(aligned(part * 32, 32), 32)], hop_recv.at[part])

            def step(s, carry):
                tc, dz, dy = (s + core) % 2, (s // 2) % 8, s // 16
                ty, tz = part * 2 + (y + dy) % 2, (z + sign * dz + 8) % 8
                place = part * 32 + (ty % 2) * 16 + tz * 2 + tc
                copy_to(source.at[place], recv.at[h], send_sem, recv_sem, device_at(plane, ty, tz, tc), me)
                return carry

            lax.fori_loop(0, 32, step, 0)
            return carry

        lax.fori_loop(0, 4, one_part, 0)

    @pl.when(x % 2 == 0)
    def _():
        all_parts(send.at[plane - 2 * half], False)

    @pl.when(x % 2 == 1)
    def _():
        all_parts(stage, True)


def finish_spread(stage, send_sem):
    x, y, z, core = coordinates()
    plane = way_back()[3]

    @pl.when(plane == x)
    def _():
        wait_for(stage.at[pl.ds(0, 127)], send_sem)

    @pl.when(plane != x)
    def _():
        wait_for(stage, send_sem)


def rows_of(ref, row):
    return ref[pl.ds(row, 128, stride=16), :]


def load_row(ref, i):
    return jnp.concatenate([rows_of(ref, i), rows_of(ref, 8 + i)], axis=1)


def store_row(ref, i, value):
    ref[pl.ds(i, 128, stride=16), :] = value[:, :128]
    ref[pl.ds(8 + i, 128, stride=16), :] = value[:, 128:]


def mean0(value):
    return jnp.sum(value, axis=0, keepdims=True) * (1.0 / value.shape[0])


def standardize(value):
    centred = value - mean0(value)
    inv_std = lax.rsqrt(mean0(centred * centred) + EPSILON)
    return centred * inv_std, inv_std


def standardize_back(scaled, normed, inv_std):
    return inv_std * (scaled - mean0(scaled) - normed * mean0(scaled * normed))


def wide(column):
    return jnp.concatenate([column, column], axis=1)


NN, NT = ((1,), (0,)), ((1,), (1,))


def neighbours():
    x, y, z, core = coordinates()
    in_z = [device_at(x, y, (z + d // 2) % NZ, (core + d) % 2) for d in range(1, 2 * NZ)]
    in_y = [device_at(x, (y + d) % NY, z, core) for d in range(1, NY)]
    in_x = [device_at((x + d) % NX, y, z, core) for d in range(1, NX)]
    return in_z, in_y, in_x


def greet(targets, sem):
    for target in targets:
        pl.semaphore_signal(sem, inc=1, device_id=target, device_id_type=MESH)


def front_row(r, i):
    z_hat, z_inv = standardize(r.pair[i].astype(jnp.float32).T)
    r.z_hat[i] = z_hat
    r.z_inv[pl.ds(i, 1)] = z_inv
    normed = (z_hat * wide(r.in_gain[...]) + wide(r.in_bias[...])).astype(jnp.bfloat16)
    r.normed[i] = normed
    proj = dot(r.proj_t[...], normed, NN)
    mask = r.mask[pl.ds(i, 1)]
    for t, rows in ((0, r.rows_a), (1, r.rows_b)):
        value, gate = proj[t * 256 : t * 256 + 128], proj[t * 256 + 128 : t * 256 + 256]
        sig = jax.nn.sigmoid(gate)
        r.value[i, t] = value
        r.sig[i, t] = sig
        store_row(rows, i, mask * sig * value)
    r.gating[i] = jax.nn.sigmoid(proj[512:])


def middle_row(r, i):
    x_hat, x_inv = standardize(load_row(r.rows_a, i))
    gain = wide(r.out_gain[...])
    xn = (x_hat * gain + wide(r.out_bias[...])).astype(jnp.bfloat16)
    r.xn[i] = xn
    projected = dot(r.out_t[...], xn, NN)
    gating, upstream = r.gating[i], r.upstream[i]
    r.update_t[i] = gating * projected
    d_proj_out = (upstream * gating).astype(jnp.bfloat16)
    r.d_proj_out[i] = d_proj_out
    r.d_gate[i] = (upstream * projected * gating * (1.0 - gating)).astype(jnp.bfloat16)
    d_xn = dot(r.out_w[...], d_proj_out, NN)
    r.out_scale[...] += d_xn * x_hat
    r.out_shift[...] += d_xn
    store_row(r.rows_b, i, standardize_back(d_xn * gain, x_hat, x_inv))


def back_row(r, i, t, rows):
    d_factor = load_row(rows, i) * r.mask[pl.ds(i, 1)]
    value, sig = r.value[i, t], r.sig[i, t]
    d_value = (d_factor * sig).astype(jnp.bfloat16)
    d_gate = (d_factor * value * sig * (1.0 - sig)).astype(jnp.bfloat16)
    d_proj = jnp.concatenate([d_value, d_gate], axis=0)
    r.part[pl.ds(t * 256, 256)] += dot(d_proj, r.normed[i], NT)
    return r.d_normed[i] + dot(r.proj_w[:, t * 256 : t * 256 + 256], d_proj, NN)


def left_row(r, i):
    r.d_normed[i] = back_row(r, i, 0, r.rows_a)


def right_row(r, i):
    d_normed = back_row(r, i, 1, r.rows_b)
    r.d_normed[i] = d_normed
    r.in_scale[...] += d_normed * r.z_hat[i]
    r.in_shift[...] += d_normed


def grad_row(r, i):
    scaled = r.d_normed[i] * wide(r.in_gain[...])
    result = standardize_back(scaled, r.z_hat[i], r.z_inv[pl.ds(i, 1)])
    r.grad_pair[i] = result.T.astype(jnp.bfloat16)


def over_rows(function, r):
    def step(i, carry):
        function(r, i)
        return carry

    lax.fori_loop(0, 8, step, 0)


def to_f32_rows(rows, tiles):
    rows[...] = tiles.astype(jnp.float32).reshape(2048, 128)


def to_tiles(rows):
    return rows[...].astype(jnp.bfloat16).reshape(128, 16, 128)


def channel_sums(value):
    return jnp.sum((value[:, :128] + value[:, 128:]).T, axis=0, keepdims=True)


def prepare(r):
    row, rep = lax.axis_index("row"), lax.axis_index("rep")
    r.proj_t[...] = r.proj_w[...].astype(jnp.float32).T.astype(jnp.bfloat16)
    r.out_t[...] = r.out_w[...].astype(jnp.float32).T.astype(jnp.bfloat16)
    for column, vector in (
        (r.in_gain, r.in_gain_row), (r.in_bias, r.in_bias_row), (r.out_gain, r.out_gain_row), (r.out_bias, r.out_bias_row),
    ):
        column[...] = jnp.broadcast_to(vector[...], (128, 128)).T
    cols = jnp.concatenate([r.mask_cols[pl.ds(rep * 2, 1)], r.mask_cols[pl.ds(rep * 2 + 1, 1)]], axis=1)
    cols = cols.astype(jnp.float32)
    for i in range(8):
        r.mask[pl.ds(i, 1)] = cols * r.mask_rows[row * 8 + i].astype(jnp.float32)


def enter(r):
    in_z, in_y, in_x = neighbours()
    barrier = pltpu.get_barrier_semaphore()
    greet(in_z + in_y + in_x, barrier)
    prepare(r)

    def step(i, carry):
        front_row(r, i)
        return carry

    lax.fori_loop(0, 4, step, 0)
    pl.semaphore_wait(barrier, len(in_z) + len(in_y) + len(in_x))
    greet(in_y, r.plane_sem)
    lax.fori_loop(4, 8, step, 0)
    pl.semaphore_wait(r.plane_sem, len(in_y))
    greet(in_x, r.all_sem)
    r.send_r[...] = to_tiles(r.rows_b)
    r.send_l[...] = to_tiles(r.rows_a)
    pl.semaphore_wait(r.all_sem, len(in_x))


def swap_right(r):
    row, rep = lax.axis_index("row"), lax.axis_index("rep")
    mine = r.recv_r.at[row % 2]
    return remote(mine, mine, r.sem.at[2], r.sem.at[3], (row + 1 - 2 * (row % 2), rep))


def send_factors(r):
    row, rep = lax.axis_index("row"), lax.axis_index("rep")
    half, slot = row // 64, rep * 64 + row % 64
    send_to_owners(r.send_r, r.recv_r.at[half, slot], r.sem.at[0], r.sem.at[1])
    send_to_owners(r.send_l, r.recv_l.at[slot], r.sem.at[16], r.sem.at[17], 0, 32)

    @pl.when((row // 32) % 2 == 0)
    def _():
        wait_for(r.recv_r.at[row % 2], r.sem.at[1])
        swap_right(r).start()

    send_to_owners(r.send_l, r.recv_l.at[slot], r.sem.at[16], r.sem.at[17], 32, 128)


def own_product(r):
    x, y, z, core = coordinates()
    rep = lax.axis_index("rep")

    def build(half):
        def step(k, carry):
            rows = pl.ds(aligned(half * 512, 512), 512)
            slots = pl.ds(aligned(k * 64, 64), 64)
            r.right[k, rows] = unpack(r.recv_r[half, slots]).astype(jnp.bfloat16)
            return carry

        lax.fori_loop(0, 4, step, 0)

    def build_left(k, carry):
        r.left[k] = unpack(r.recv_l[pl.ds(aligned(k * 64, 64), 64)]).astype(jnp.bfloat16)
        return carry

    build(core)
    swap_right(r).wait()
    build(1 - core)
    wait_for(r.recv_l, r.sem.at[17])
    lax.fori_loop(0, 4, build_left, 0)

    def result(q, carry):
        part = turn(q, 1 - 2 * ((x // 2 + core) % 2), rep)
        rows = pl.ds(aligned(part * 256, 256), 256)
        total = dot(r.left[0], r.right[0, rows], NT)
        for k in range(1, 4):
            total += dot(r.left[k], r.right[k, rows], NT)
        r.back_p[:, pl.ds(aligned(part * 32, 32), 32)] = pack(total)
        start_hop(r.back_p, r.stage_p, part, r.sem.at[4], r.hop_p)
        return carry

    lax.fori_loop(0, 4, result, 0)
    left_swap(r).start()


def left_swap(r):
    row, rep = lax.axis_index("row"), lax.axis_index("rep")
    return remote(r.left, r.left_other, r.sem.at[5], r.sem.at[6], (row + 1 - 2 * (row % 2), rep))


def own_gradients(r):
    x, y, z, core = coordinates()
    row, rep = lax.axis_index("row"), lax.axis_index("rep")
    wait_for(r.recv_d, r.sem.at[8])
    crossing = remote(
        r.recv_d.at[pl.ds(aligned((1 - core) * 128, 128), 128)],
        r.cross, r.sem.at[9], r.sem.at[10], (row + 1 - 2 * core, rep),
    )
    crossing.start()

    def build(k, carry):
        r.d_own[k] = unpack(r.recv_d[pl.ds(aligned(k * 64, 64), 64)]).astype(jnp.bfloat16)
        return carry

    lax.fori_loop(0, 4, build, 0)
    def for_left(q, carry):
        part = turn(q, 1 - 2 * ((x // 2 + core) % 2), rep)
        total = dot(r.d_own[0], r.right[part, pl.ds(0, 256)], NN)
        for k in range(1, 4):
            total += dot(r.d_own[k], r.right[part, pl.ds(k * 256, 256)], NN)
        r.back_l[:, pl.ds(aligned(part * 32, 32), 32)] = pack(total)
        start_hop(r.back_l, r.stage_l, part, r.sem.at[11], r.hop_l)
        return carry

    lax.fori_loop(0, 4, for_left, 0)
    for a in range(2):
        slots = pl.ds(aligned(core * 128 + a * 64, 64), 64)
        r.d_mine[a] = unpack(r.recv_d[slots]).T.astype(jnp.bfloat16)
    crossing.wait()
    for a in range(2):
        r.d_cross[a] = unpack(r.cross[pl.ds(a * 64, 64)]).T.astype(jnp.bfloat16)
    left_swap(r).wait()

    def for_right(q, carry):
        part = turn(q, 1 - 2 * ((x // 2 + core) % 2), rep)
        totals = [
            dot(r.d_mine[a], r.left[part], NN) + dot(r.d_cross[a], r.left_other[part], NN) for a in range(2)
        ]
        r.back_r[:, pl.ds(aligned(part * 32, 32), 32)] = pack(jnp.concatenate(totals, axis=0))
        start_hop(r.back_r, r.stage_r, part, r.sem.at[18], r.hop_r)
        return carry

    lax.fori_loop(0, 4, for_right, 0)


def sum_over_devices(r, meanwhile):
    x, y, z, core = coordinates()
    row, rep = lax.axis_index("row"), lax.axis_index("rep")
    sibling = (row + 1 - 2 * core, rep)
    sends, recvs = r.sum_send, r.sum_recv

    def at(base, start, size):
        return base.at[pl.ds(aligned(start, 8), size)]

    first = remote(at(r.part, (1 - core) * 512, 512), r.from_core, sends.at[0], recvs.at[0], sibling)
    first.start()
    first.wait_recv()
    r.half[...] = r.part[pl.ds(aligned(core * 512, 512), 512)] + r.from_core[...]

    r.from_z[z] = r.half[pl.ds(aligned(z * 64, 64), 64)]
    for dz in range(1, NZ):
        tz = (z + dz) % NZ
        remote(
            at(r.half, tz * 64, 64), r.from_z.at[z], sends.at[1], recvs.at[1], device_at(x, y, tz, core)
        ).start()
    meanwhile()
    wait_for(r.from_z.at[pl.ds(0, NZ - 1)], recvs.at[1])
    r.z_sum[...] = jnp.sum(r.from_z[...], axis=0)

    r.from_xy[x * NY + y] = r.z_sum[pl.ds(aligned(y * 8, 8), 8)]
    for d in range(1, NX * NY):
        tx, ty = (x + d // NY) % NX, (y + d % NY) % NY
        remote(
            at(r.z_sum, ty * 8, 8), r.from_xy.at[x * NY + y], sends.at[2], recvs.at[2], device_at(tx, ty, z, core)
        ).start()
    wait_for(r.from_xy.at[pl.ds(0, NX * NY - 1)], recvs.at[2])
    r.xy_sum[...] = jnp.sum(r.from_xy[...], axis=0)

    r.y_rows[y] = r.xy_sum[...]
    for dy in range(1, NY):
        remote(
            r.xy_sum, r.y_rows.at[y], sends.at[3], recvs.at[3], device_at(x, (y + dy) % NY, z, core)
        ).start()
    wait_for(r.y_rows.at[pl.ds(0, NY - 1)], recvs.at[3])

    r.z_part[...] = r.y_rows[...].reshape(64, 128).astype(jnp.bfloat16)
    r.z_rows[z] = r.z_part[...]
    for dz in range(1, NZ):
        remote(
            r.z_part, r.z_rows.at[z], sends.at[4], recvs.at[4], device_at(x, y, (z + dz) % NZ, core)
        ).start()
    wait_for(r.z_rows.at[pl.ds(0, NZ - 1)], recvs.at[4])

    r.both[core] = r.z_rows[...]
    last = remote(r.z_rows, r.both.at[core], sends.at[5], recvs.at[5], sibling)
    last.start()
    last.wait()
    total = r.both[...].reshape(1024, 128).astype(jnp.float32) * (1.0 / r.mask_rows.shape[0])
    for b in range(5):
        r.grad_proj[:, b * 128 : (b + 1) * 128] = total[b * 128 : (b + 1) * 128].T
    r.grad_out[...] = total[640:768]
    r.grad_in_norm[...] = total[768:770]
    r.grad_out_norm[...] = total[770:772]

    first.wait_send()
    wait_for(r.from_z.at[pl.ds(0, NZ - 1)], sends.at[1])
    wait_for(r.from_xy.at[pl.ds(0, NX * NY - 1)], sends.at[2])
    wait_for(r.y_rows.at[pl.ds(0, NY - 1)], sends.at[3])
    wait_for(r.z_rows.at[pl.ds(0, NZ - 1)], sends.at[4])


def step_kernel(names, *refs):
    r = types.SimpleNamespace(**dict(zip(names, refs)))
    x, y, z, core = coordinates()
    row, rep = lax.axis_index("row"), lax.axis_index("rep")
    owner = x % 2 == 0

    enter(r)
    send_factors(r)

    def turn_cotangent(r, i):
        r.upstream[i] = r.cotangent[i].astype(jnp.float32).T

    over_rows(turn_cotangent, r)
    for name in ("part", "out_scale", "out_shift", "in_scale", "in_shift"):
        ref = getattr(r, name)
        ref[...] = jnp.zeros(ref.shape, ref.dtype)

    @pl.when(owner)
    def _():
        own_product(r)

    spread(r.back_p, r.stage_p, r.recv_p, r.hop_p, r.sem.at[12], r.sem.at[13])
    wait_for(r.recv_p, r.sem.at[13])

    to_f32_rows(r.rows_a, r.recv_p[...])
    over_rows(middle_row, r)
    r.send_d[...] = to_tiles(r.rows_b)
    send_to_owners(r.send_d, r.recv_d.at[rep * 64 + row % 64], r.sem.at[7], r.sem.at[8])

    def finish_middle(r, i):
        r.update[i] = r.update_t[i].T.astype(jnp.bfloat16)
        d_gate = r.d_gate[i]
        r.part[pl.ds(512, 128)] += dot(d_gate, r.normed[i], NT)
        r.part[pl.ds(640, 128)] += dot(r.xn[i], r.d_proj_out[i], NT)
        r.d_normed[i] = dot(r.proj_w[:, 512:], d_gate, NN)

    over_rows(finish_middle, r)

    @pl.when(owner)
    def _():
        own_gradients(r)

    spread(r.back_l, r.stage_l, r.recv_gl, r.hop_l, r.sem.at[14], r.sem.at[15])
    spread(r.back_r, r.stage_r, r.recv_gr, r.hop_r, r.sem.at[19], r.sem.at[20])
    wait_for(r.recv_gl, r.sem.at[15])
    to_f32_rows(r.rows_a, r.recv_gl[...])
    over_rows(left_row, r)
    wait_for(r.recv_gr, r.sem.at[20])
    to_f32_rows(r.rows_b, r.recv_gr[...])
    over_rows(right_row, r)
    norms = [channel_sums(ref[...]) for ref in (r.in_scale, r.in_shift, r.out_scale, r.out_shift)]
    r.part[pl.ds(768, 8)] = jnp.concatenate(norms + [jnp.zeros((4, 128), jnp.float32)], axis=0)

    sum_over_devices(r, lambda: over_rows(grad_row, r))

    finish_sends(r.send_r, r.sem.at[0])
    finish_sends(r.send_l, r.sem.at[16])
    finish_sends(r.send_d, r.sem.at[7])
    finish_spread(r.stage_p, r.sem.at[12])
    finish_spread(r.stage_l, r.sem.at[14])
    finish_spread(r.stage_r, r.sem.at[19])

    @pl.when(owner)
    def _():
        finish_hop(r.back_p, r.sem.at[4])
        finish_hop(r.back_l, r.sem.at[11])
        finish_hop(r.back_r, r.sem.at[18])


VMEM = pl.BlockSpec(memory_space=pltpu.VMEM)
DMA = pltpu.SemaphoreType.DMA


def scratch():
    f32, bf16 = jnp.float32, jnp.bfloat16

    def of(dtype, *shape):
        return pltpu.VMEM(shape, dtype)

    return {
        "rows_a": of(f32, 2048, 128),
        "rows_b": of(f32, 2048, 128),
        "z_hat": of(f32, 8, 128, 256),
        "z_inv": of(f32, 8, 256),
        "normed": of(bf16, 8, 128, 256),
        "value": of(f32, 8, 2, 128, 256),
        "sig": of(f32, 8, 2, 128, 256),
        "gating": of(f32, 8, 128, 256),
        "upstream": of(f32, 8, 128, 256),
        "xn": of(bf16, 8, 128, 256),
        "update_t": of(f32, 8, 128, 256),
        "d_proj_out": of(bf16, 8, 128, 256),
        "d_gate": of(bf16, 8, 128, 256),
        "mask": of(f32, 8, 256),
        "in_gain": of(f32, 128, 128),
        "in_bias": of(f32, 128, 128),
        "out_gain": of(f32, 128, 128),
        "out_bias": of(f32, 128, 128),
        "proj_t": of(bf16, 640, 128),
        "out_t": of(bf16, 128, 128),
        "d_normed": of(f32, 8, 128, 256),
        "out_scale": of(f32, 128, 256),
        "out_shift": of(f32, 128, 256),
        "in_scale": of(f32, 128, 256),
        "in_shift": of(f32, 128, 256),
        "send_l": of(bf16, 128, 16, 128),
        "send_r": of(bf16, 128, 16, 128),
        "recv_l": of(bf16, 256, 16, 128),
        "recv_r": of(bf16, 2, 256, 16, 128),
        "left": of(bf16, 4, 512, 256),
        "right": of(bf16, 4, 1024, 256),
        "back_p": of(bf16, 2, 128, 16, 128),
        "stage_p": of(bf16, 128, 16, 128),
        "recv_p": of(bf16, 128, 16, 128),
        "send_d": of(bf16, 128, 16, 128),
        "recv_d": of(bf16, 256, 16, 128),
        "left_other": of(bf16, 4, 512, 256),
        "cross": of(bf16, 128, 16, 128),
        "d_own": of(bf16, 4, 512, 256),
        "d_mine": of(bf16, 2, 256, 512),
        "d_cross": of(bf16, 2, 256, 512),
        "back_l": of(bf16, 2, 128, 16, 128),
        "back_r": of(bf16, 2, 128, 16, 128),
        "stage_l": of(bf16, 128, 16, 128),
        "stage_r": of(bf16, 128, 16, 128),
        "recv_gl": of(bf16, 128, 16, 128),
        "recv_gr": of(bf16, 128, 16, 128),
        "part": of(f32, 1024, 128),
        "from_core": of(f32, 512, 128),
        "half": of(f32, 512, 128),
        "from_z": of(f32, 8, 64, 128),
        "z_sum": of(f32, 64, 128),
        "from_xy": of(f32, 32, 8, 128),
        "xy_sum": of(f32, 8, 128),
        "y_rows": of(f32, 8, 8, 128),
        "z_part": of(bf16, 64, 128),
        "z_rows": of(bf16, 8, 64, 128),
        "both": of(bf16, 2, 8, 64, 128),
        "sem": DMA((21,)),
        "hop_p": DMA((4,)),
        "hop_l": DMA((4,)),
        "hop_r": DMA((4,)),
        "plane_sem": pltpu.SemaphoreType.REGULAR,
        "all_sem": pltpu.SemaphoreType.REGULAR,
        "sum_send": DMA((6,)),
        "sum_recv": DMA((6,)),
    }


INPUTS = (
    "mask_rows", "mask_cols", "pair", "cotangent", "in_gain_row", "in_bias_row", "out_gain_row", "out_bias_row",
    "proj_w", "out_w",
)
OUTPUTS = ("update", "grad_pair", "grad_proj", "grad_out", "grad_in_norm", "grad_out_norm")


def whole_step(*args):
    extra = scratch()
    names = INPUTS + OUTPUTS + tuple(extra)
    block = jax.ShapeDtypeStruct((8, 256, 128), jnp.bfloat16)

    def weights(*shape):
        return jax.ShapeDtypeStruct(shape, jnp.float32)

    return pl.pallas_call(
        functools.partial(step_kernel, names),
        out_shape=(block, block, weights(128, 640), weights(128, 128), weights(2, 128), weights(2, 128)),
        in_specs=[pl.BlockSpec(memory_space=pltpu.SMEM)] + [VMEM] * (len(INPUTS) - 1),
        out_specs=(VMEM,) * len(OUTPUTS),
        scratch_shapes=list(extra.values()),
        compiler_params=pltpu.CompilerParams(
            has_side_effects=True, collective_id=0, vmem_limit_bytes=56 << 20
        ),
        name="triangle_step",
    )(*args)


def body(
    pair, cotangent, token_mask, in_gain, in_bias, proj_weight, out_gain, out_bias, out_weight
):
    return whole_step(
        token_mask,
        token_mask.reshape(8, 128),
        pair,
        cotangent,
        *[v.reshape(1, 128) for v in (in_gain, in_bias, out_gain, out_bias)],
        proj_weight,
        out_weight,
    )


def solution(mesh):
    in_specs = (P("row", "rep", None), P("row", "rep", None), P(), P(), P(), P(), P(), P(), P())
    out_specs = (P("row", "rep", None), P("row", "rep", None), P(), P(), P(), P())
    return jax.shard_map(body, mesh=mesh, in_specs=in_specs, out_specs=out_specs, check_vma=False)
```

```python
import functools
import types

import jax
import jax.numpy as jnp
from jax import lax
from jax.experimental import pallas as pl
from jax.experimental.pallas import tpu as pltpu
from jax.sharding import PartitionSpec as P

EPSILON = 1e-05
MESH = pl.DeviceIdType.MESH
NX, NY, NZ = 4, 8, 8


def coordinates():
    row, rep = lax.axis_index("row"), lax.axis_index("rep")
    return row // 32, rep * 2 + (row // 16) % 2, (row // 2) % 8, row % 2


def device_at(x, y, z, core):
    return (((x * 2 + y % 2) * 8 + z) * 2 + core, y // 2)


def remote(src, dst, send_sem, recv_sem, target):
    return pltpu.make_async_remote_copy(
        src, dst, send_sem, recv_sem, device_id=target, device_id_type=MESH
    )


def copy_to(src, dst, send_sem, recv_sem, target, me):
    same = jnp.logical_and(target[0] == me[0], target[1] == me[1])

    @pl.when(same)
    def _():
        pltpu.make_async_copy(src, dst, recv_sem).start()

    @pl.when(jnp.logical_not(same))
    def _():
        remote(src, dst, send_sem, recv_sem, target).start()


def wait_for(ref, sem):
    pltpu.make_async_copy(ref, ref, sem).wait()


def send_to_owners(send, place, send_sem, recv_sem, first=0, last=128):
    x, y, z, core = coordinates()
    me = (lax.axis_index("row"), lax.axis_index("rep"))
    sign = 1 - 2 * core

    def step(s, carry):
        dz, dy, dx = s % 8, (s // 8) % 8, s // 64
        hx = (x // 2 + dx) % 2
        ty, tz = (y + sign * dy + 8) % 8, (z + sign * dz + 8) % 8
        h = hx * 64 + ty * 8 + tz
        copy_to(send.at[h], place, send_sem, recv_sem, device_at(2 * hx, ty, tz, x // 2), me)
        return carry

    lax.fori_loop(first, last, step, 0)


def finish_sends(send, send_sem):
    x, y, z, core = coordinates()
    keeps = jnp.logical_and(x % 2 == 0, core == x // 2)

    @pl.when(keeps)
    def _():
        wait_for(send.at[pl.ds(0, 127)], send_sem)

    @pl.when(jnp.logical_not(keeps))
    def _():
        wait_for(send, send_sem)


def aligned(start, unit):
    return pl.multiple_of(start, unit)


def unpack(slots):
    wide = slots.astype(jnp.float32)
    low, high = wide[:, :8].reshape(512, 128), wide[:, 8:].reshape(512, 128)
    return jnp.concatenate([low, high], axis=1)


def pack(block):
    low, high = block[:, :128].reshape(64, 8, 128), block[:, 128:].reshape(64, 8, 128)
    return jnp.concatenate([low, high], axis=1).astype(jnp.bfloat16).reshape(2, 32, 16, 128)


def dot(a, b, contract):
    return lax.dot_general(a, b, ((contract[0], contract[1]), ((), ())), preferred_element_type=jnp.float32)


def turn(q, sign, rep):
    return (rep + sign * q + 4) % 4


def way_back():
    x, y, z, core = coordinates()
    even = x % 2 == 0
    hx = jnp.where(even, x // 2, core)
    half = jnp.where(even, core, x // 2)
    differ = (hx + half) % 2
    plane = jnp.where(even, (x + 3 * differ) % 4, 2 * half + 1 - differ)
    return hx, half, differ, plane


def start_hop(send, stage, part, hop_send, hop_recv):
    x, y, z, core = coordinates()
    hx, half, differ, plane = way_back()
    rows = pl.ds(aligned(part * 32, 32), 32)
    target = device_at((x + 1 + 2 * differ) % 4, y, z, hx)
    other = 1 - (plane - 2 * half)
    remote(send.at[other, rows], stage.at[rows], hop_send, hop_recv.at[part], target).start()


def finish_hop(send, hop_send):
    wait_for(send.at[0], hop_send)


def spread(send, stage, recv, hop_recv, send_sem, recv_sem, in_turns=True):
    x, y, z, core = coordinates()
    rep = lax.axis_index("rep")
    me = (lax.axis_index("row"), rep)
    hx, half, differ, plane = way_back()
    h = hx * 64 + y * 8 + z
    sign = 1 - 2 * core

    def all_parts(source, staged):
        def one_part(q, carry):
            part = turn(q, 1 - 2 * differ, rep)
            if staged:
                wait_for(source.at[pl.ds(aligned(part * 32, 32), 32)], hop_recv.at[part])

            def step(s, carry):
                tc, dz, dy = (s + core) % 2, (s // 2) % 8, s // 16
                ty, tz = part * 2 + (y + dy) % 2, (z + sign * dz + 8) % 8
                place = part * 32 + (ty % 2) * 16 + tz * 2 + tc
                copy_to(source.at[place], recv.at[h], send_sem, recv_sem, device_at(plane, ty, tz, tc), me)
                return carry

            lax.fori_loop(0, 32, step, 0)
            return carry

        lax.fori_loop(0, 4, one_part, 0)

    def at_once(source):
        def step(s, carry):
            tc, dy, dz = (s // 64 + core) % 2, (s // 8) % 8, s % 8
            ty, tz = (y + sign * dy + 8) % 8, (z + sign * dz + 8) % 8
            place = ty * 16 + tz * 2 + tc
            copy_to(source.at[place], recv.at[h], send_sem, recv_sem, device_at(plane, ty, tz, tc), me)
            return carry

        lax.fori_loop(0, 128, step, 0)

    @pl.when(x % 2 == 0)
    def _():
        source = send.at[plane - 2 * half]
        if in_turns:
            all_parts(source, False)
        else:
            at_once(source)

    @pl.when(x % 2 == 1)
    def _():
        if in_turns:
            all_parts(stage, True)
        else:
            for part in range(4):
                wait_for(stage.at[pl.ds(part * 32, 32)], hop_recv.at[part])
            at_once(stage)


def finish_spread(stage, send_sem):
    x, y, z, core = coordinates()
    plane = way_back()[3]

    @pl.when(plane == x)
    def _():
        wait_for(stage.at[pl.ds(0, 127)], send_sem)

    @pl.when(plane != x)
    def _():
        wait_for(stage, send_sem)


def rows_of(ref, row):
    return ref[pl.ds(row, 128, stride=16), :]


def load_row(ref, i):
    return jnp.concatenate([rows_of(ref, i), rows_of(ref, 8 + i)], axis=1)


def store_row(ref, i, value):
    ref[pl.ds(i, 128, stride=16), :] = value[:, :128]
    ref[pl.ds(8 + i, 128, stride=16), :] = value[:, 128:]


def mean0(value):
    return jnp.sum(value, axis=0, keepdims=True) * (1.0 / value.shape[0])


def standardize(value):
    centred = value - mean0(value)
    inv_std = lax.rsqrt(mean0(centred * centred) + EPSILON)
    return centred * inv_std, inv_std


def standardize_back(scaled, normed, inv_std):
    return inv_std * (scaled - mean0(scaled) - normed * mean0(scaled * normed))


def wide(column):
    return jnp.concatenate([column, column], axis=1)


NN, NT = ((1,), (0,)), ((1,), (1,))


def neighbours():
    x, y, z, core = coordinates()
    in_z = [device_at(x, y, (z + d // 2) % NZ, (core + d) % 2) for d in range(1, 2 * NZ)]
    in_y = [device_at(x, (y + d) % NY, z, core) for d in range(1, NY)]
    in_x = [device_at((x + d) % NX, y, z, core) for d in range(1, NX)]
    return in_z, in_y, in_x


def greet(targets, sem):
    for target in targets:
        pl.semaphore_signal(sem, inc=1, device_id=target, device_id_type=MESH)


def front_row(r, i):
    z_hat, z_inv = standardize(r.pair[i].astype(jnp.float32).T)
    r.z_hat[i] = z_hat
    r.z_inv[pl.ds(i, 1)] = z_inv
    normed = (z_hat * wide(r.in_gain[...]) + wide(r.in_bias[...])).astype(jnp.bfloat16)
    r.normed[i] = normed
    proj = dot(r.proj_t[...], normed, NN)
    mask = r.mask[pl.ds(i, 1)]
    for t, rows in ((0, r.rows_a), (1, r.rows_b)):
        value, gate = proj[t * 256 : t * 256 + 128], proj[t * 256 + 128 : t * 256 + 256]
        sig = jax.nn.sigmoid(gate)
        r.value[i, t] = value
        r.sig[i, t] = sig
        store_row(rows, i, mask * sig * value)
    r.gating[i] = jax.nn.sigmoid(proj[512:])


def middle_row(r, i):
    x_hat, x_inv = standardize(load_row(r.rows_a, i))
    gain = wide(r.out_gain[...])
    xn = (x_hat * gain + wide(r.out_bias[...])).astype(jnp.bfloat16)
    r.xn[i] = xn
    projected = dot(r.out_t[...], xn, NN)
    gating, upstream = r.gating[i], r.upstream[i]
    r.update_t[i] = gating * projected
    d_proj_out = (upstream * gating).astype(jnp.bfloat16)
    r.d_proj_out[i] = d_proj_out
    r.d_gate[i] = (upstream * projected * gating * (1.0 - gating)).astype(jnp.bfloat16)
    d_xn = dot(r.out_w[...], d_proj_out, NN)
    r.out_scale[...] += d_xn * x_hat
    r.out_shift[...] += d_xn
    store_row(r.rows_b, i, standardize_back(d_xn * gain, x_hat, x_inv))


def back_row(r, i, t, rows):
    d_factor = load_row(rows, i) * r.mask[pl.ds(i, 1)]
    value, sig = r.value[i, t], r.sig[i, t]
    d_value = (d_factor * sig).astype(jnp.bfloat16)
    d_gate = (d_factor * value * sig * (1.0 - sig)).astype(jnp.bfloat16)
    d_proj = jnp.concatenate([d_value, d_gate], axis=0)
    r.part[pl.ds(t * 256, 256)] += dot(d_proj, r.normed[i], NT)
    return r.d_normed[i] + dot(r.proj_w[:, t * 256 : t * 256 + 256], d_proj, NN)


def left_row(r, i):
    r.d_normed[i] = back_row(r, i, 0, r.rows_a)


def right_row(r, i):
    d_normed = back_row(r, i, 1, r.rows_b)
    r.d_normed[i] = d_normed
    r.in_scale[...] += d_normed * r.z_hat[i]
    r.in_shift[...] += d_normed


def grad_row(r, i):
    scaled = r.d_normed[i] * wide(r.in_gain[...])
    result = standardize_back(scaled, r.z_hat[i], r.z_inv[pl.ds(i, 1)])
    r.grad_pair[i] = result.T.astype(jnp.bfloat16)


def over_rows(function, r):
    def step(i, carry):
        function(r, i)
        return carry

    lax.fori_loop(0, 8, step, 0)


def to_f32_rows(rows, tiles):
    rows[...] = tiles.astype(jnp.float32).reshape(2048, 128)


def to_tiles(rows):
    return rows[...].astype(jnp.bfloat16).reshape(128, 16, 128)


def channel_sums(value):
    return jnp.sum((value[:, :128] + value[:, 128:]).T, axis=0, keepdims=True)


def prepare(r):
    row, rep = lax.axis_index("row"), lax.axis_index("rep")
    r.proj_t[...] = r.proj_w[...].astype(jnp.float32).T.astype(jnp.bfloat16)
    r.out_t[...] = r.out_w[...].astype(jnp.float32).T.astype(jnp.bfloat16)
    for column, vector in (
        (r.in_gain, r.in_gain_row), (r.in_bias, r.in_bias_row), (r.out_gain, r.out_gain_row), (r.out_bias, r.out_bias_row),
    ):
        column[...] = jnp.broadcast_to(vector[...], (128, 128)).T
    cols = jnp.concatenate([r.mask_cols[pl.ds(rep * 2, 1)], r.mask_cols[pl.ds(rep * 2 + 1, 1)]], axis=1)
    cols = cols.astype(jnp.float32)
    for i in range(8):
        r.mask[pl.ds(i, 1)] = cols * r.mask_rows[row * 8 + i].astype(jnp.float32)


def enter(r):
    in_z, in_y, in_x = neighbours()
    barrier = pltpu.get_barrier_semaphore()
    greet(in_z + in_y + in_x, barrier)
    prepare(r)

    def step(i, carry):
        front_row(r, i)
        return carry

    lax.fori_loop(0, 4, step, 0)
    pl.semaphore_wait(barrier, len(in_z) + len(in_y) + len(in_x))
    greet(in_y, r.plane_sem)
    lax.fori_loop(4, 8, step, 0)
    pl.semaphore_wait(r.plane_sem, len(in_y))
    greet(in_x, r.all_sem)
    r.send_r[...] = to_tiles(r.rows_b)
    r.send_l[...] = to_tiles(r.rows_a)
    pl.semaphore_wait(r.all_sem, len(in_x))


def swap_right(r):
    row, rep = lax.axis_index("row"), lax.axis_index("rep")
    mine = r.recv_r.at[row % 2]
    return remote(mine, mine, r.sem.at[2], r.sem.at[3], (row + 1 - 2 * (row % 2), rep))


def send_factors(r):
    row, rep = lax.axis_index("row"), lax.axis_index("rep")
    half, slot = row // 64, rep * 64 + row % 64
    send_to_owners(r.send_r, r.recv_r.at[half, slot], r.sem.at[0], r.sem.at[1])
    send_to_owners(r.send_l, r.recv_l.at[slot], r.sem.at[16], r.sem.at[17], 0, 32)

    @pl.when((row // 32) % 2 == 0)
    def _():
        wait_for(r.recv_r.at[row % 2], r.sem.at[1])
        swap_right(r).start()

    send_to_owners(r.send_l, r.recv_l.at[slot], r.sem.at[16], r.sem.at[17], 32, 128)


def own_product(r):
    x, y, z, core = coordinates()
    rep = lax.axis_index("rep")

    def build(half):
        def step(k, carry):
            rows = pl.ds(aligned(half * 512, 512), 512)
            slots = pl.ds(aligned(k * 64, 64), 64)
            r.right[k, rows] = unpack(r.recv_r[half, slots]).astype(jnp.bfloat16)
            return carry

        lax.fori_loop(0, 4, step, 0)

    def build_left(k, carry):
        r.left[k] = unpack(r.recv_l[pl.ds(aligned(k * 64, 64), 64)]).astype(jnp.bfloat16)
        return carry

    build(core)
    swap_right(r).wait()
    build(1 - core)
    wait_for(r.recv_l, r.sem.at[17])
    lax.fori_loop(0, 4, build_left, 0)

    def result(q, carry):
        part = turn(q, 1 - 2 * ((x // 2 + core) % 2), rep)
        rows = pl.ds(aligned(part * 256, 256), 256)
        total = dot(r.left[0], r.right[0, rows], NT)
        for k in range(1, 4):
            total += dot(r.left[k], r.right[k, rows], NT)
        r.back_p[:, pl.ds(aligned(part * 32, 32), 32)] = pack(total)
        start_hop(r.back_p, r.stage_p, part, r.sem.at[4], r.hop_p)
        return carry

    lax.fori_loop(0, 4, result, 0)
    left_swap(r).start()


def left_swap(r):
    row, rep = lax.axis_index("row"), lax.axis_index("rep")
    return remote(r.left, r.left_other, r.sem.at[5], r.sem.at[6], (row + 1 - 2 * (row % 2), rep))


def own_gradients(r):
    x, y, z, core = coordinates()
    row, rep = lax.axis_index("row"), lax.axis_index("rep")
    wait_for(r.recv_d, r.sem.at[8])
    crossing = remote(
        r.recv_d.at[pl.ds(aligned((1 - core) * 128, 128), 128)],
        r.cross, r.sem.at[9], r.sem.at[10], (row + 1 - 2 * core, rep),
    )
    crossing.start()

    def build(k, carry):
        r.d_own[k] = unpack(r.recv_d[pl.ds(aligned(k * 64, 64), 64)]).astype(jnp.bfloat16)
        return carry

    lax.fori_loop(0, 4, build, 0)
    def for_left(q, carry):
        part = turn(q, 1 - 2 * ((x // 2 + core) % 2), rep)
        total = dot(r.d_own[0], r.right[part, pl.ds(0, 256)], NN)
        for k in range(1, 4):
            total += dot(r.d_own[k], r.right[part, pl.ds(k * 256, 256)], NN)
        r.back_l[:, pl.ds(aligned(part * 32, 32), 32)] = pack(total)
        start_hop(r.back_l, r.stage_l, part, r.sem.at[11], r.hop_l)
        return carry

    lax.fori_loop(0, 4, for_left, 0)
    for a in range(2):
        slots = pl.ds(aligned(core * 128 + a * 64, 64), 64)
        r.d_mine[a] = unpack(r.recv_d[slots]).T.astype(jnp.bfloat16)
    crossing.wait()
    for a in range(2):
        r.d_cross[a] = unpack(r.cross[pl.ds(a * 64, 64)]).T.astype(jnp.bfloat16)
    left_swap(r).wait()

    def for_right(q, carry):
        part = turn(q, 1 - 2 * ((x // 2 + core) % 2), rep)
        totals = [
            dot(r.d_mine[a], r.left[part], NN) + dot(r.d_cross[a], r.left_other[part], NN) for a in range(2)
        ]
        r.back_r[:, pl.ds(aligned(part * 32, 32), 32)] = pack(jnp.concatenate(totals, axis=0))
        start_hop(r.back_r, r.stage_r, part, r.sem.at[18], r.hop_r)
        return carry

    lax.fori_loop(0, 4, for_right, 0)


def sum_over_devices(r, meanwhile):
    x, y, z, core = coordinates()
    row, rep = lax.axis_index("row"), lax.axis_index("rep")
    sibling = (row + 1 - 2 * core, rep)
    sends, recvs = r.sum_send, r.sum_recv

    def at(base, start, size):
        return base.at[pl.ds(aligned(start, 8), size)]

    first = remote(at(r.part, (1 - core) * 512, 512), r.from_core, sends.at[0], recvs.at[0], sibling)
    first.start()
    first.wait_recv()
    r.half[...] = r.part[pl.ds(aligned(core * 512, 512), 512)] + r.from_core[...]

    r.from_z[z] = r.half[pl.ds(aligned(z * 64, 64), 64)]
    for dz in range(1, NZ):
        tz = (z + dz) % NZ
        remote(
            at(r.half, tz * 64, 64), r.from_z.at[z], sends.at[1], recvs.at[1], device_at(x, y, tz, core)
        ).start()
    meanwhile()
    wait_for(r.from_z.at[pl.ds(0, NZ - 1)], recvs.at[1])
    r.z_sum[...] = jnp.sum(r.from_z[...], axis=0)

    r.from_xy[x * NY + y] = r.z_sum[pl.ds(aligned(y * 8, 8), 8)]
    for d in range(1, NX * NY):
        tx, ty = (x + d // NY) % NX, (y + d % NY) % NY
        remote(
            at(r.z_sum, ty * 8, 8), r.from_xy.at[x * NY + y], sends.at[2], recvs.at[2], device_at(tx, ty, z, core)
        ).start()
    wait_for(r.from_xy.at[pl.ds(0, NX * NY - 1)], recvs.at[2])
    r.xy_sum[...] = jnp.sum(r.from_xy[...], axis=0)

    r.y_rows[y] = r.xy_sum[...]
    for dy in range(1, NY):
        remote(
            r.xy_sum, r.y_rows.at[y], sends.at[3], recvs.at[3], device_at(x, (y + dy) % NY, z, core)
        ).start()
    wait_for(r.y_rows.at[pl.ds(0, NY - 1)], recvs.at[3])

    r.z_part[...] = r.y_rows[...].reshape(64, 128).astype(jnp.bfloat16)
    r.z_rows[z] = r.z_part[...]
    for dz in range(1, NZ):
        remote(
            r.z_part, r.z_rows.at[z], sends.at[4], recvs.at[4], device_at(x, y, (z + dz) % NZ, core)
        ).start()
    wait_for(r.z_rows.at[pl.ds(0, NZ - 1)], recvs.at[4])

    r.both[core] = r.z_rows[...]
    last = remote(r.z_rows, r.both.at[core], sends.at[5], recvs.at[5], sibling)
    last.start()
    last.wait()
    total = r.both[...].reshape(1024, 128).astype(jnp.float32) * (1.0 / r.mask_rows.shape[0])
    for b in range(5):
        r.grad_proj[:, b * 128 : (b + 1) * 128] = total[b * 128 : (b + 1) * 128].T
    r.grad_out[...] = total[640:768]
    r.grad_in_norm[...] = total[768:770]
    r.grad_out_norm[...] = total[770:772]

    first.wait_send()
    wait_for(r.from_z.at[pl.ds(0, NZ - 1)], sends.at[1])
    wait_for(r.from_xy.at[pl.ds(0, NX * NY - 1)], sends.at[2])
    wait_for(r.y_rows.at[pl.ds(0, NY - 1)], sends.at[3])
    wait_for(r.z_rows.at[pl.ds(0, NZ - 1)], sends.at[4])


def step_kernel(names, *refs):
    r = types.SimpleNamespace(**dict(zip(names, refs)))
    x, y, z, core = coordinates()
    row, rep = lax.axis_index("row"), lax.axis_index("rep")
    owner = x % 2 == 0

    enter(r)
    send_factors(r)

    def turn_cotangent(r, i):
        r.upstream[i] = r.cotangent[i].astype(jnp.float32).T

    over_rows(turn_cotangent, r)
    for name in ("part", "out_scale", "out_shift", "in_scale", "in_shift"):
        ref = getattr(r, name)
        ref[...] = jnp.zeros(ref.shape, ref.dtype)

    @pl.when(owner)
    def _():
        own_product(r)

    spread(r.back_p, r.stage_p, r.recv_p, r.hop_p, r.sem.at[12], r.sem.at[13])
    wait_for(r.recv_p, r.sem.at[13])

    to_f32_rows(r.rows_a, r.recv_p[...])
    over_rows(middle_row, r)
    r.send_d[...] = to_tiles(r.rows_b)
    send_to_owners(r.send_d, r.recv_d.at[rep * 64 + row % 64], r.sem.at[7], r.sem.at[8])

    def finish_middle(r, i):
        r.update[i] = r.update_t[i].T.astype(jnp.bfloat16)
        d_gate = r.d_gate[i]
        r.part[pl.ds(512, 128)] += dot(d_gate, r.normed[i], NT)
        r.part[pl.ds(640, 128)] += dot(r.xn[i], r.d_proj_out[i], NT)
        r.d_normed[i] = dot(r.proj_w[:, 512:], d_gate, NN)

    over_rows(finish_middle, r)

    @pl.when(owner)
    def _():
        own_gradients(r)

    spread(r.back_l, r.stage_l, r.recv_gl, r.hop_l, r.sem.at[14], r.sem.at[15])
    spread(r.back_r, r.stage_r, r.recv_gr, r.hop_r, r.sem.at[19], r.sem.at[20], in_turns=False)
    wait_for(r.recv_gl, r.sem.at[15])
    to_f32_rows(r.rows_a, r.recv_gl[...])
    over_rows(left_row, r)
    wait_for(r.recv_gr, r.sem.at[20])
    to_f32_rows(r.rows_b, r.recv_gr[...])
    over_rows(right_row, r)
    norms = [channel_sums(ref[...]) for ref in (r.in_scale, r.in_shift, r.out_scale, r.out_shift)]
    r.part[pl.ds(768, 8)] = jnp.concatenate(norms + [jnp.zeros((4, 128), jnp.float32)], axis=0)

    sum_over_devices(r, lambda: over_rows(grad_row, r))

    finish_sends(r.send_r, r.sem.at[0])
    finish_sends(r.send_l, r.sem.at[16])
    finish_sends(r.send_d, r.sem.at[7])
    finish_spread(r.stage_p, r.sem.at[12])
    finish_spread(r.stage_l, r.sem.at[14])
    finish_spread(r.stage_r, r.sem.at[19])

    @pl.when(owner)
    def _():
        finish_hop(r.back_p, r.sem.at[4])
        finish_hop(r.back_l, r.sem.at[11])
        finish_hop(r.back_r, r.sem.at[18])


VMEM = pl.BlockSpec(memory_space=pltpu.VMEM)
DMA = pltpu.SemaphoreType.DMA


def scratch():
    f32, bf16 = jnp.float32, jnp.bfloat16

    def of(dtype, *shape):
        return pltpu.VMEM(shape, dtype)

    return {
        "rows_a": of(f32, 2048, 128),
        "rows_b": of(f32, 2048, 128),
        "z_hat": of(f32, 8, 128, 256),
        "z_inv": of(f32, 8, 256),
        "normed": of(bf16, 8, 128, 256),
        "value": of(f32, 8, 2, 128, 256),
        "sig": of(f32, 8, 2, 128, 256),
        "gating": of(f32, 8, 128, 256),
        "upstream": of(f32, 8, 128, 256),
        "xn": of(bf16, 8, 128, 256),
        "update_t": of(f32, 8, 128, 256),
        "d_proj_out": of(bf16, 8, 128, 256),
        "d_gate": of(bf16, 8, 128, 256),
        "mask": of(f32, 8, 256),
        "in_gain": of(f32, 128, 128),
        "in_bias": of(f32, 128, 128),
        "out_gain": of(f32, 128, 128),
        "out_bias": of(f32, 128, 128),
        "proj_t": of(bf16, 640, 128),
        "out_t": of(bf16, 128, 128),
        "d_normed": of(f32, 8, 128, 256),
        "out_scale": of(f32, 128, 256),
        "out_shift": of(f32, 128, 256),
        "in_scale": of(f32, 128, 256),
        "in_shift": of(f32, 128, 256),
        "send_l": of(bf16, 128, 16, 128),
        "send_r": of(bf16, 128, 16, 128),
        "recv_l": of(bf16, 256, 16, 128),
        "recv_r": of(bf16, 2, 256, 16, 128),
        "left": of(bf16, 4, 512, 256),
        "right": of(bf16, 4, 1024, 256),
        "back_p": of(bf16, 2, 128, 16, 128),
        "stage_p": of(bf16, 128, 16, 128),
        "recv_p": of(bf16, 128, 16, 128),
        "send_d": of(bf16, 128, 16, 128),
        "recv_d": of(bf16, 256, 16, 128),
        "left_other": of(bf16, 4, 512, 256),
        "cross": of(bf16, 128, 16, 128),
        "d_own": of(bf16, 4, 512, 256),
        "d_mine": of(bf16, 2, 256, 512),
        "d_cross": of(bf16, 2, 256, 512),
        "back_l": of(bf16, 2, 128, 16, 128),
        "back_r": of(bf16, 2, 128, 16, 128),
        "stage_l": of(bf16, 128, 16, 128),
        "stage_r": of(bf16, 128, 16, 128),
        "recv_gl": of(bf16, 128, 16, 128),
        "recv_gr": of(bf16, 128, 16, 128),
        "part": of(f32, 1024, 128),
        "from_core": of(f32, 512, 128),
        "half": of(f32, 512, 128),
        "from_z": of(f32, 8, 64, 128),
        "z_sum": of(f32, 64, 128),
        "from_xy": of(f32, 32, 8, 128),
        "xy_sum": of(f32, 8, 128),
        "y_rows": of(f32, 8, 8, 128),
        "z_part": of(bf16, 64, 128),
        "z_rows": of(bf16, 8, 64, 128),
        "both": of(bf16, 2, 8, 64, 128),
        "sem": DMA((21,)),
        "hop_p": DMA((4,)),
        "hop_l": DMA((4,)),
        "hop_r": DMA((4,)),
        "plane_sem": pltpu.SemaphoreType.REGULAR,
        "all_sem": pltpu.SemaphoreType.REGULAR,
        "sum_send": DMA((6,)),
        "sum_recv": DMA((6,)),
    }


INPUTS = (
    "mask_rows", "mask_cols", "pair", "cotangent", "in_gain_row", "in_bias_row", "out_gain_row", "out_bias_row",
    "proj_w", "out_w",
)
OUTPUTS = ("update", "grad_pair", "grad_proj", "grad_out", "grad_in_norm", "grad_out_norm")


def whole_step(*args):
    extra = scratch()
    names = INPUTS + OUTPUTS + tuple(extra)
    block = jax.ShapeDtypeStruct((8, 256, 128), jnp.bfloat16)

    def weights(*shape):
        return jax.ShapeDtypeStruct(shape, jnp.float32)

    return pl.pallas_call(
        functools.partial(step_kernel, names),
        out_shape=(block, block, weights(128, 640), weights(128, 128), weights(2, 128), weights(2, 128)),
        in_specs=[pl.BlockSpec(memory_space=pltpu.SMEM)] + [VMEM] * (len(INPUTS) - 1),
        out_specs=(VMEM,) * len(OUTPUTS),
        scratch_shapes=list(extra.values()),
        compiler_params=pltpu.CompilerParams(
            has_side_effects=True, collective_id=0, vmem_limit_bytes=56 << 20
        ),
        name="triangle_step",
    )(*args)


def body(
    pair, cotangent, token_mask, in_gain, in_bias, proj_weight, out_gain, out_bias, out_weight
):
    return whole_step(
        token_mask,
        token_mask.reshape(8, 128),
        pair,
        cotangent,
        *[v.reshape(1, 128) for v in (in_gain, in_bias, out_gain, out_bias)],
        proj_weight,
        out_weight,
    )


def solution(mesh):
    in_specs = (P("row", "rep", None), P("row", "rep", None), P(), P(), P(), P(), P(), P(), P())
    out_specs = (P("row", "rep", None), P("row", "rep", None), P(), P(), P(), P())
    return jax.shard_map(body, mesh=mesh, in_specs=in_specs, out_specs=out_specs, check_vma=False)
```
